768 devices in a mesh: lat: 192 (over z, y_hi, x, core), lon: 4 (over y_lo).
Axes of the slice: x: 4, y: 8 (y_hi: 2, y_lo: 4; y = y_hi * 4 + y_lo), z: 12, core: 2. Of those that a mesh axis runs over, the one named last changes fastest.
Arguments:
- lam_end: float32 [4, 16, 1536, 512], P(None, None, 'lat', 'lon'), may hold values from -6 to 6
- winds: float32 [2, 16, 1536, 512], P(None, None, 'lat', 'lon'), may hold values from -0.5 to 0.5
- coupling: float32 [4, 16, 1536, 512], P(None, None, 'lat', 'lon'), may hold values from -0.5 to 0.5
- obs_values: float32 [768, 4, 64, 128], P(('lat', 'lon')), may hold values from -6 to 6
- obs_column: int32 [768, 4, 64], P(('lat', 'lon')), may hold values from 0 to 1023
- obs_count: int32 [768, 4], P(('lat', 'lon')), may hold values from 8 to 64, as said below
Outputs:
- gradient: float32 [4, 16, 1536, 512], P(None, None, 'lat', 'lon')
The draws below stay inside these ranges and needn't reach their ends.
Inputs may be any that keep to these rules, and one draw needn't show every extreme that they name: `obs_column`: target column of a slot within its destination tile, numbered latitude row times 128 plus longitude column, in the sender's own latitude band; targets may repeat, and padding slots hold targets too. `obs_count`: slots from this count on are padding. In every latitude band some destination tile, drawn from the seed, gets 64 live slots from every device of the band.
All inputs are finite; a program needn't handle non-finite values.
Results may differ from the reference program's by a relative error of at most 0.00002.
Values sent between devices are 32-bit elements; how exact they have to be, the bound alone decides.
No kernel may reach another device: no remote copies, remote signals or barrier semaphores. Data moves between devices by JAX's collectives and lax.ppermute only.
A program may use at most 32 MiB of HBM per device.

```python
import jax
import jax.numpy as jnp
from jax import lax

LEV = 16
STEPS = 4
CLAT = 8
CLON = 128
CAP = 64
BLOCK = 128
BANDS = 192
TILES = 4
SENDERS = 768
NLAT = 1536
NLON = 512


def draw_obs_count(key, part):
    key = jax.random.fold_in(key, 11)
    dense_key, base_key = jax.random.split(key)
    dense_tile = jax.random.randint(dense_key, (BANDS,), 0, TILES)
    base_count = jax.random.randint(base_key, (BANDS, TILES, TILES), CAP // 8, CAP // 4 + 1)
    hot_tile = jnp.arange(TILES, dtype=jnp.int32)[None, None, :] == dense_tile[:, None, None]
    return jnp.where(hot_tile, CAP, base_count).reshape(SENDERS, TILES).astype(jnp.int32)


def plant(values, own_key, low, top_value):
    place = [jax.random.randint(jax.random.fold_in(own_key, axis), (), 0, length) for axis, length in enumerate(values.shape)]
    longest = values.shape.index(max(values.shape))
    neighbour = place[:longest] + [(place[longest] + 1) % values.shape[longest]] + place[longest + 1:]
    return values.at[tuple(place)].set(low).at[tuple(neighbour)].set(top_value)


def block_levels(own_key, dims, cuts, least, largest):
    gain = 1.0
    for dim, shards_of in cuts:
        steps = jax.random.uniform(jax.random.fold_in(jax.random.fold_in(own_key, 6), dim), (shards_of,), jnp.float32, least / len(cuts), largest / len(cuts))
        gain = gain * jnp.repeat(jnp.exp(steps), dims[dim] // shards_of).reshape((-1,) + (1,) * (len(dims) - 1 - dim))
    return gain


def normal_values(stream_key, shape, scale, reach, cuts=(), kind=jnp.bfloat16):
    values = jax.random.normal(stream_key, shape, jnp.float32) * scale
    if len(cuts) > 0:
        values = block_levels(stream_key, shape, cuts, -0.22, 0.18) * values
    return jnp.clip(values, min=-reach, max=reach).astype(kind)


def setup_inputs(seed: int = 0) -> dict:
    streams_of = jax.random.split(jax.random.key(seed), 7)
    lam_end = normal_values(streams_of[0], (4, LEV, NLAT, NLON), 1.0, 6.0, ((2, 192), (3, 4)), jnp.float32)
    winds = jnp.clip(jax.random.uniform(streams_of[1], (2, LEV, NLAT, NLON), jnp.float32, -0.5, 0.5) * block_levels(streams_of[1], (2, LEV, NLAT, NLON), ((2, 192), (3, 4)), -0.4, 0.0), -0.5, 0.5)
    coupling = jnp.clip(jax.random.uniform(streams_of[2], (4, LEV, NLAT, NLON), jnp.float32, -0.5, 0.5) * block_levels(streams_of[2], (4, LEV, NLAT, NLON), ((2, 192), (3, 4)), -0.4, 0.0), -0.5, 0.5)
    obs_values = normal_values(streams_of[3], (SENDERS, TILES, CAP, BLOCK), 1.0, 6.0, ((0, 768),), jnp.float32)
    obs_column = plant(jax.random.randint(streams_of[4], (SENDERS, TILES, CAP), 0, CLAT * CLON), jax.random.fold_in(streams_of[4], 1), 0, (CLAT * CLON) - 1).astype(jnp.int32)
    obs_count = draw_obs_count(jax.random.fold_in(streams_of[6], 71), 0)
    return dict(lam_end=lam_end, winds=winds, coupling=coupling, obs_values=obs_values, obs_column=obs_column, obs_count=obs_count)


DIFFUSION = 0.1


def adjoint_step(padded, lat_wind, lon_wind, coupling):
    lat_flux = lat_wind * padded
    lon_flux = lon_wind * padded
    centre = padded[..., 1:-1, 1:-1]
    upper = padded[..., 2:, 1:-1]
    lower = padded[..., :-2, 1:-1]
    right_side = padded[..., 1:-1, 2:]
    left_side = padded[..., 1:-1, :-2]
    advect = 0.5 * (lat_flux[..., 2:, 1:-1] - lat_flux[..., :-2, 1:-1] + lon_flux[..., 1:-1, 2:] - lon_flux[..., 1:-1, :-2])
    updated = centre + advect + DIFFUSION * (upper + lower + right_side + left_side - 4.0 * centre)
    couple_centre = coupling[..., 1:-1, 1:-1]
    wind_lat = updated[0] - (couple_centre[0] * centre[2] + couple_centre[2] * centre[3])
    wind_lon = updated[1] - (couple_centre[1] * centre[2] + couple_centre[3] * centre[3])
    return jnp.stack([wind_lat, wind_lon, updated[2], updated[3]])


def extend(quantity):
    wrapped = jnp.concatenate([quantity[..., -1:], quantity, quantity[..., :1]], axis=-1)
    widths = [(0, 0)] * (quantity.ndim - 2) + [(1, 1), (0, 0)]
    return jnp.pad(wrapped, widths)


def reference(lam_end, winds, coupling, obs_values, obs_column, obs_count):
    grid_lat = CLAT * BANDS
    grid_lon = CLON * TILES
    band_index = jnp.arange(SENDERS, dtype=jnp.int32) // TILES
    tile_index = jnp.arange(TILES, dtype=jnp.int32)
    target_row = obs_column // CLON
    target_col = obs_column % CLON
    global_row = band_index[:, None, None] * CLAT + target_row
    global_col = tile_index[None, :, None] * CLON + target_col
    target = (global_row * grid_lon + global_col).reshape(-1).astype(jnp.int32)
    live_slots = jnp.arange(CAP, dtype=jnp.int32)[None, None, :] < obs_count[:, :, None]
    blocks = (obs_values * live_slots[..., None].astype(obs_values.dtype)).reshape(-1, STEPS, 2, LEV)
    by_level = jnp.moveaxis(blocks, 3, 0)

    def per_level(level_items):
        level_values, adjoint, wind_level, couple_level = level_items
        summed = jax.ops.segment_sum(level_values.reshape(-1, STEPS * 2), target, num_segments=grid_lat * grid_lon)
        forcing = summed.T.reshape(STEPS, 2, grid_lat, grid_lon)
        wind_ext = extend(wind_level)
        couple_ext = extend(couple_level)
        for instant in range(STEPS):
            slot_time = STEPS - 1 - instant
            adjoint = jnp.concatenate([adjoint[:2], adjoint[2:] + forcing[slot_time]])
            adjoint = adjoint_step(extend(adjoint), wind_ext[0], wind_ext[1], couple_ext)
        return adjoint

    result = lax.map(per_level, (by_level, jnp.moveaxis(lam_end, 1, 0), jnp.moveaxis(winds, 1, 0), jnp.moveaxis(coupling, 1, 0)))
    return jnp.moveaxis(result, 0, 1)
```

```python
import functools

import jax
import jax.numpy as jnp
from jax import lax
from jax.experimental import pallas as pl
from jax.experimental.pallas import tpu as pltpu
from jax.sharding import PartitionSpec as P

DIFFUSION = 0.1
F32 = jnp.float32
BF16 = jnp.bfloat16

TARGET_ROW = 64
EDGE_ROW = 72
STRIP_ROW = 136
LON_ROWS = 216

A_AT, B_AT, C_AT, STRIP_AT = 16, 18, 19, 23
LAT_ROWS = 25 * 16
CENTRE = 1.0 - 4.0 * DIFFUSION


def pieces(values):
    high = values.astype(BF16)
    rest = values - high.astype(F32)
    middle = rest.astype(BF16)
    low = (rest - middle.astype(F32)).astype(BF16)
    return high, middle, low


def lanes_of(rows):
    return lax.broadcasted_iota(jnp.int32, (rows, 128), 1)


def levels(ref, field, row, first=0, count=16):
    return ref[field, pl.ds(first * 8 + row, count, stride=8), :]


def pack_kernel(*refs):
    sources, out_ref, copies_of, sems = refs[:6], refs[6], refs[7:13], refs[13]
    copies = [pltpu.make_async_copy(sources[i], copies_of[i], sems.at[i]) for i in range(6)]
    for copy in copies:
        copy.start()
    for copy in copies[:3]:
        copy.wait()
    count_ref, column_ref, values_ref, lam_ref, winds_ref, coupling_ref = copies_of
    slot = lax.broadcasted_iota(jnp.int32, (64, 128), 0)
    blocks = []
    columns = []
    for tile in range(4):
        block = jnp.where(slot < count_ref[0, tile], values_ref[tile], 0.0)
        blocks.append(block)
        column = column_ref[tile : tile + 1, :]
        columns.append(column)
        out_ref[tile, 0:64, :] = block
        wide = jnp.concatenate([column, jnp.zeros((1, 64), jnp.int32)], axis=1)
        out_ref[tile, TARGET_ROW:EDGE_ROW, :] = jnp.broadcast_to(wide.astype(F32), (8, 128))

    cell = lax.broadcasted_iota(jnp.int32, (64, 128), 0)
    side = cell & 7
    wanted = (cell >> 3) * 128 + jnp.where(side < 4, 124 + side, side - 4)
    allowed = (lanes_of(64) < 64) == (side < 4)
    for tile in range(4):
        left, right = (tile + 3) % 4, (tile + 1) % 4
        target = jnp.concatenate([columns[left], columns[right]], axis=1)
        hit = jnp.where(jnp.logical_and(jnp.broadcast_to(target, (64, 128)) == wanted, allowed), 1.0, 0.0)
        hit = hit.astype(BF16)
        both = jnp.concatenate([blocks[left], blocks[right]], axis=0)
        total = jnp.zeros((64, 128), F32)
        for piece in pieces(both):
            total = total + jnp.dot(hit, piece, preferred_element_type=F32)
        out_ref[tile, EDGE_ROW:STRIP_ROW, :] = total

    for copy in copies[3:]:
        copy.wait()
    lane = lanes_of(8)
    row = STRIP_ROW
    for ref, fields in ((lam_ref, 4), (winds_ref, 2), (coupling_ref, 4)):
        for field in range(fields):
            strip = jnp.zeros((8, 128), F32)
            for half in range(2):
                for r in range(8):
                    at = half * 64 + r * 8
                    moved = pltpu.roll(levels(ref, field, r, half * 8, 8), (at + 4) % 128, 1)
                    strip = jnp.where(jnp.logical_and(lane >= at, lane < at + 8), moved, strip)
            for tile in range(4):
                out_ref[tile, row : row + 8, :] = strip
            row += 8


def strip_lane(plane, way):
    return ((plane % 16) * 8 + way * (88 if plane == A_AT + 1 else 72)) % 128


def once(make):
    made = {}

    def get(*key):
        if key not in made:
            made[key] = make(*key)
        return made[key]

    return get


def along(x, to_left, to_right, beside, at, lane):
    p_right, p_left = to_left * x, to_right * x
    edge = pltpu.roll(beside, (128 - (at + 4)) % 128, 1)
    right = jnp.where(lane == 127, edge, pltpu.roll(p_right, 127, 1))
    left = jnp.where(lane == 0, edge, pltpu.roll(p_left, 1, 1))
    return right + left, jnp.where(lane == 0, p_right, p_left)


def insert(inner, pair, at, lane):
    moved = pltpu.roll(pair, (at + 4) % 128, 1)
    return jnp.where(jnp.logical_or(lane == at + 4, lane == at + 3), moved, inner)


def strip_along(rolled_right, rolled_left, inner, side):
    right = jnp.where(side == 3, pltpu.roll(inner, 127, 1), rolled_right)
    left = jnp.where(side == 4, pltpu.roll(inner, 1, 1), rolled_left)
    return right + left


def own_steps(lam_ref, winds_ref, coupling_ref, force_ref, strips_ref, wanted, keep):
    lane = lanes_of(8)
    side = lane & 7
    strip_row = (lane >> 3) & 7

    def force(row, instant, field, half):
        at = instant * 32 + field * 16 + half * 8
        return force_ref[row, at : at + 8, :]

    half_wind = once(lambda axis, row, half: 0.5 * levels(winds_ref, axis, row, half * 8, 8))
    up_weight = once(lambda row, half: DIFFUSION + half_wind(0, row, half))
    down_weight = once(lambda row, half: DIFFUSION - half_wind(0, row, half))
    right_weight = once(lambda row, half: DIFFUSION + half_wind(1, row, half))
    left_weight = once(lambda row, half: DIFFUSION - half_wind(1, row, half))

    def strip(place):
        return strips_ref[place * 8 : place * 8 + 8, :]

    half_a, half_b = 0.5 * strip(4), 0.5 * strip(5)
    strip_up, strip_down = DIFFUSION + half_a, DIFFUSION - half_a
    strip_right, strip_left = DIFFUSION + half_b, DIFFUSION - half_b

    u = [{}, {}, {}, {}]
    for field in range(4):
        for half in range(2):
            for row in range(8):
                value = levels(lam_ref, field, row, half * 8, 8)
                if field >= 2:
                    value = value + force(row, 3, field - 2, half)
                u[field][row, half] = value
    strips = [strip(field) for field in range(4)]
    keep(0, u, strips)
    for step, rows in enumerate(wanted, 1):
        last = step == 4
        later = [{}, {}, {}, {}]
        later_strips = []
        for field in range(4):
            x = u[field]
            rolled_right = pltpu.roll(strip_right * strips[field], 127, 1)
            rolled_left = pltpu.roll(strip_left * strips[field], 1, 1)
            beside = jnp.where(side == 3, rolled_right, rolled_left)
            inner = beside
            for half in range(2):
                for row in rows:
                    at = half * 64 + row * 8
                    shares, pair = along(
                        x[row, half], right_weight(row, half), left_weight(row, half), beside, at, lane
                    )
                    total = CENTRE * x[row, half] + shares
                    if row < 7:
                        total = total + up_weight(row + 1, half) * x[row + 1, half]
                    if row > 0:
                        total = total + down_weight(row - 1, half) * x[row - 1, half]
                    if field < 2:
                        first = levels(coupling_ref, field, row, half * 8, 8)
                        second = levels(coupling_ref, field + 2, row, half * 8, 8)
                        total = total - (first * u[2][row, half] + second * u[3][row, half])
                    elif not last:
                        total = total + force(row, 3 - step, field - 2, half)
                    later[field][row, half] = total
                    if not last:
                        inner = insert(inner, pair, at, lane)
            if not last:
                total = CENTRE * strips[field] + strip_along(rolled_right, rolled_left, inner, side)
                total = total + jnp.where(strip_row == 7, 0.0, pltpu.roll(strip_up * strips[field], 120, 1))
                total = total + jnp.where(strip_row == 0, 0.0, pltpu.roll(strip_down * strips[field], 8, 1))
                if field < 2:
                    total = total - (strip(6 + field) * strips[2] + strip(8 + field) * strips[3])
                else:
                    total = total + strip(10 + 2 * (step - 1) + field - 2)
                later_strips.append(total)
        u, strips = later, later_strips
        keep(step, u, strips)


def halo_kernel(place_ref, got_ref, lam_ref, winds_ref, coupling_ref, even_ref, odd_ref, force_ref, strips_ref):
    is_even = lax.rem(place_ref[0], 2) == 0
    tile = place_ref[1]
    lane = lanes_of(8)
    lane1 = lanes_of(1)

    rows = [got_ref[s, TARGET_ROW : TARGET_ROW + 1, :] for s in range(4)]
    halves = [jnp.where(lane1 < 64, rows[s], pltpu.roll(rows[s + 1], 64, 1)) for s in (0, 2)]
    target = jnp.concatenate(halves, axis=1).astype(jnp.int32)
    blocks = jnp.concatenate([got_ref[s, 0:64, :] for s in range(4)], axis=0)
    stacked = jnp.concatenate(pieces(blocks.T), axis=0)
    cell = lax.broadcasted_iota(jnp.int32, (256, 256), 0)
    for pair in range(4):
        hit = jnp.where(jnp.broadcast_to(target, (256, 256)) == cell + pair * 256, 1.0, 0.0).astype(BF16)
        three = lax.dot_general(stacked, hit, (((1,), (1,)), ((), ())), preferred_element_type=F32)
        both = three[0:128] + three[128:256] + three[256:384]
        force_ref[2 * pair] = both[:, 0:128]
        force_ref[2 * pair + 1] = both[:, 128:256]

    edge = got_ref[0, EDGE_ROW:STRIP_ROW, :]
    for s in range(1, 4):
        edge = edge + got_ref[s, EDGE_ROW:STRIP_ROW, :]
    edge = jnp.concatenate([edge, edge], axis=0).T

    def edge_strip(instant, field):
        at = instant * 32 + field * 16
        return jnp.where(lane < 64, edge[at : at + 8], edge[at + 8 : at + 16])

    left = lax.rem(tile + 3, 4)
    right = lax.rem(tile + 1, 4)
    for field in range(10):
        at = STRIP_ROW + field * 8
        strip = jnp.where((lane & 7) < 4, got_ref[left, at : at + 8, :], got_ref[right, at : at + 8, :])
        if field in (2, 3):
            strip = strip + edge_strip(3, field - 2)
        strips_ref[field * 8 : field * 8 + 8, :] = strip
    for place, (instant, field) in enumerate(((2, 0), (2, 1), (1, 0), (1, 1), (0, 0), (0, 1))):
        strips_ref[80 + place * 8 : 88 + place * 8, :] = edge_strip(instant, field)

    sides = {}

    def put(plane, half, up, down):
        at = plane * 16 + half * 8
        even_ref[at : at + 8, :] = jnp.where(is_even, up, down)
        odd_ref[at : at + 8, :] = jnp.where(is_even, down, up)

    def put_strip(plane, packed, up_row, down_row):
        for half in range(2):
            for way, row in ((0, up_row), (1, down_row)):
                at = strip_lane(plane, way)
                mine = jnp.logical_and(lane >= at, lane < at + 8)
                key = (STRIP_AT + plane // 16, half, way)
                moved = pltpu.roll(packed, (at - half * 64 - row * 8) % 128, 1)
                sides[key] = jnp.where(mine, moved, sides.get(key, 0.0))

    def keep(step, u, strips):
        for field in range(4):
            plane = step * 4 + field
            for half in range(2):
                put(plane, half, u[field][7, half], u[field][0, half])
            if step < 3:
                put_strip(plane, strips[field], 7, 0)

    own_steps(
        lam_ref,
        winds_ref,
        coupling_ref,
        force_ref,
        strips_ref,
        ((0, 1, 2, 5, 6, 7), (0, 1, 6, 7), (0, 7)),
        keep,
    )
    for plane, ref, field, depth in (
        (A_AT, winds_ref, 0, 0),
        (A_AT + 1, winds_ref, 0, 1),
        (B_AT, winds_ref, 1, 0),
        (C_AT, coupling_ref, 0, 0),
        (C_AT + 1, coupling_ref, 1, 0),
        (C_AT + 2, coupling_ref, 2, 0),
        (C_AT + 3, coupling_ref, 3, 0),
    ):
        for half in range(2):
            put(plane, half, levels(ref, field, 7 - depth, half * 8, 8), levels(ref, field, depth, half * 8, 8))
        place = field + (4 if ref is winds_ref else 6)
        put_strip(plane, strips_ref[place * 8 : place * 8 + 8, :], 7 - depth, depth)
    for plane in (STRIP_AT, STRIP_AT + 1):
        for half in range(2):
            put(plane, half, sides[plane, half, 0], sides[plane, half, 1])


def own_kernel(force_ref, strips_ref, lam_ref, winds_ref, coupling_ref, out_ref, wide_ref):
    every = tuple(range(8))

    def widen(place, packed):
        for half in range(2):
            at = (place * 2 + half) * 8
            wide_ref[at : at + 8, :] = pltpu.roll(packed, 16 if half == 0 else 80, 1)

    def keep(step, u, strips):
        for field in range(4):
            if step < 3:
                widen(step * 4 + field, strips[field])
            if step == 4:
                for half in range(2):
                    for row in range(8):
                        out_ref[field, row, half * 8 : half * 8 + 8, :] = u[field][row, half]

    for place in range(6):
        widen(12 + place, strips_ref[32 + place * 8 : 40 + place * 8, :])
    own_steps(lam_ref, winds_ref, coupling_ref, force_ref, strips_ref, (every,) * 4, keep)


def join_kernel(
    place_ref,
    odd_ref,
    even_ref,
    sent_odd_ref,
    sent_even_ref,
    own_ref,
    wide_ref,
    winds_ref,
    coupling_ref,
    out_ref,
    border_ref,
):
    band = place_ref[0]
    is_even = lax.rem(band, 2) == 0
    low_mask = jnp.where(band > 0, 1.0, 0.0).astype(F32)
    high_mask = jnp.where(band < place_ref[2] - 1, 1.0, 0.0).astype(F32)
    lane = lanes_of(8)
    side = lane & 7
    strip_row = (lane >> 3) - 2
    strip_mask = jnp.where(strip_row < 0, low_mask, jnp.where(strip_row > 7, high_mask, 1.0))

    def chosen(first, second):
        def get(plane, half):
            at = plane * 16 + half * 8
            return jnp.where(is_even, first[at : at + 8, :], second[at : at + 8, :])

        return once(get)

    low, high = chosen(odd_ref, even_ref), chosen(even_ref, odd_ref)
    up, down = chosen(sent_even_ref, sent_odd_ref), chosen(sent_odd_ref, sent_even_ref)
    border_of = {-1: low, 0: down, 7: up, 8: high}

    def outer(first, row, half, own):
        if row < 0:
            return low(first - 1 - row, half)
        if row > 7:
            return high(first + row - 8, half)
        return own

    def half_wind(axis, row, half):
        own = levels(winds_ref, axis, row, half * 8, 8) if 0 <= row <= 7 else None
        return 0.5 * outer(A_AT if axis == 0 else B_AT, row, half, own)

    half_wind = once(half_wind)
    up_weight = once(lambda row, half: DIFFUSION + half_wind(0, row, half))
    down_weight = once(lambda row, half: DIFFUSION - half_wind(0, row, half))
    right_weight = once(lambda row, half: DIFFUSION + half_wind(1, row, half))
    left_weight = once(lambda row, half: DIFFUSION - half_wind(1, row, half))

    def couple(field, row, half):
        own = levels(coupling_ref, field, row, half * 8, 8) if 0 <= row <= 7 else None
        return outer(C_AT + field, row, half, own)

    couple = once(couple)

    def met(plane, half):
        at = strip_lane(plane, 0)
        mine = jnp.logical_and(lane >= at, lane < at + 8)
        both = jnp.where(mine, low(STRIP_AT + plane // 16, half), high(STRIP_AT + plane // 16, half))
        return pltpu.roll(both, ((0 if plane == A_AT + 1 else 8) - at) % 128, 1)

    inside = jnp.logical_and(strip_row >= 0, strip_row <= 7)

    def strip(place, plane, half):
        at = (place * 2 + half) * 8
        return jnp.where(inside, wide_ref[at : at + 8, :], met(plane, half))

    for plane in range(12):
        for half in range(2):
            at = (plane * 2 + half) * 8
            border_ref[at : at + 8, :] = strip(plane, plane, half)
    deepest = jnp.logical_or(strip_row == -2, strip_row == 9)
    strip_a = [
        0.5 * jnp.where(deepest, met(A_AT + 1, half), strip(12, A_AT, half)) for half in range(2)
    ]
    strip_b = [0.5 * strip(13, B_AT, half) for half in range(2)]
    strip_c = [[strip(14 + field, C_AT + field, half) for half in range(2)] for field in range(4)]

    e = [{}, {}, {}, {}]
    strips = [[None, None] for _ in range(4)]
    reach = ((-1, 0), (-2, -1, 0, 1), (-1, 0, 1, 2), (0, 1, 2, 3))
    for step in range(4):
        last = step == 3
        rows = reach[step] + tuple(7 - row for row in reach[step])
        later = [{}, {}, {}, {}]
        later_strips = [[None, None] for _ in range(4)]
        for field in range(4):
            x = e[field]
            plane = step * 4 + field
            for half in range(2):
                xs = strips[field][half]
                if step > 0:
                    rolled_right = pltpu.roll((DIFFUSION + strip_b[half]) * xs, 127, 1)
                    rolled_left = pltpu.roll((DIFFUSION - strip_b[half]) * xs, 1, 1)
                    beside = jnp.where(side == 3, rolled_right, rolled_left)
                    inner = beside
                for row in rows:
                    terms = []
                    if (row, half) in x:
                        here = x[row, half]
                        at = (row + 2) * 8
                        shares, pair = along(
                            here, right_weight(row, half), left_weight(row, half), beside, at, lane
                        )
                        local = CENTRE * here + shares
                        if field < 2:
                            local = local - (
                                couple(field, row, half) * e[2][row, half]
                                + couple(field + 2, row, half) * e[3][row, half]
                            )
                        terms.append(local)
                        if not last:
                            inner = insert(inner, pair, at, lane)
                    for near, crossing, weight in (
                        (row + 1, (0, 8), up_weight),
                        (row - 1, (-1, 7), down_weight),
                    ):
                        parts = []
                        if (near, half) in x:
                            parts.append(x[near, half])
                        if near in crossing:
                            parts.append(border_of[near](plane, half))
                        if parts:
                            terms.append(weight(near, half) * sum(parts[1:], parts[0]))
                    total = sum(terms[1:], terms[0])
                    if row == -1:
                        total = total * low_mask
                    if row == 8:
                        total = total * high_mask
                    if last:
                        total = total + own_ref[field, row, half * 8 : half * 8 + 8, :]
                        out_ref[field, pl.ds(half * 64 + row, 8, stride=8), :] = total
                    else:
                        later[field][row, half] = total
                if not last:
                    at = (plane * 2 + half) * 8
                    border = border_ref[at : at + 8, :]
                    from_above = jnp.where(jnp.logical_or(strip_row == 0, strip_row == 8), border, 0.0)
                    from_below = jnp.where(jnp.logical_or(strip_row == -1, strip_row == 7), border, 0.0)
                    if step > 0:
                        from_above, from_below = from_above + xs, from_below + xs
                    total = pltpu.roll((DIFFUSION + strip_a[half]) * from_above, 120, 1)
                    total = total + pltpu.roll((DIFFUSION - strip_a[half]) * from_below, 8, 1)
                    if step > 0:
                        total = total + CENTRE * xs + strip_along(rolled_right, rolled_left, inner, side)
                        if field < 2:
                            total = total - (
                                strip_c[field][half] * strips[2][half] + strip_c[field + 2][half] * strips[3][half]
                            )
                    later_strips[field][half] = total * strip_mask
        e, strips = later, later_strips


def vmem(count):
    return [pl.BlockSpec(memory_space=pltpu.VMEM)] * count


SMEM = pl.BlockSpec(memory_space=pltpu.SMEM)


def params(mebibytes=24):
    return pltpu.CompilerParams(vmem_limit_bytes=mebibytes * 1024 * 1024)


def body(lam_end, winds, coupling, obs_values, obs_column, obs_count):
    bands = lax.axis_size("lat")
    tiles = lax.axis_size("lon")
    lam = lam_end.reshape(4, 128, 128)
    wind = winds.reshape(2, 128, 128)
    couple = coupling.reshape(4, 128, 128)
    place = jnp.stack([lax.axis_index("lat"), lax.axis_index("lon"), jnp.int32(bands)]).astype(jnp.int32)

    message = pl.pallas_call(
        pack_kernel,
        out_shape=jax.ShapeDtypeStruct((tiles, LON_ROWS, 128), F32),
        in_specs=[pl.BlockSpec(memory_space=pltpu.HBM)] * 6,
        out_specs=vmem(1)[0],
        scratch_shapes=[
            pltpu.SMEM((1, 4), jnp.int32),
            pltpu.VMEM((4, 64), jnp.int32),
            pltpu.VMEM((4, 64, 128), F32),
            pltpu.VMEM((4, 128, 128), F32),
            pltpu.VMEM((2, 128, 128), F32),
            pltpu.VMEM((4, 128, 128), F32),
            pltpu.SemaphoreType.DMA((6,)),
        ],
        compiler_params=params(60),
        name="pack_blocks_and_strips",
    )(obs_count, obs_column[0], obs_values[0], lam, wind, couple)
    got = lax.all_to_all(message, "lon", split_axis=0, concat_axis=0, tiled=True)

    halo = jax.ShapeDtypeStruct((LAT_ROWS, 128), F32)
    even, odd, force, strips = pl.pallas_call(
        halo_kernel,
        out_shape=(
            halo,
            halo,
            jax.ShapeDtypeStruct((8, 128, 128), F32),
            jax.ShapeDtypeStruct((128, 128), F32),
        ),
        in_specs=[SMEM] + vmem(4),
        out_specs=tuple(vmem(4)),
        compiler_params=params(),
        name="scatter_and_halo",
    )(place, got, lam, wind, couple)
    swap = lambda first: [p for i in range(first, bands - 1, 2) for p in ((i, i + 1), (i + 1, i))]
    got_odd = lax.ppermute(odd, "lat", swap(1))
    got_even = lax.ppermute(even, "lat", swap(0))

    own, wide = pl.pallas_call(
        own_kernel,
        out_shape=(jax.ShapeDtypeStruct((4, 8, 16, 128), F32), jax.ShapeDtypeStruct((288, 128), F32)),
        in_specs=vmem(5),
        out_specs=tuple(vmem(2)),
        compiler_params=params(),
        cost_estimate=pl.CostEstimate(flops=10_000_000, bytes_accessed=2_000_000, transcendentals=0),
        name="own_steps",
    )(force, strips, lam, wind, couple)

    out = pl.pallas_call(
        join_kernel,
        out_shape=jax.ShapeDtypeStruct((4, 128, 128), F32),
        in_specs=[SMEM] + vmem(8),
        out_specs=vmem(1)[0],
        scratch_shapes=[pltpu.VMEM((192, 128), F32)],
        compiler_params=params(),
        name="join_bands",
    )(place, got_odd, got_even, odd, even, own, wide, wind, couple)
    return out.reshape(lam_end.shape)


def solution(mesh):
    return jax.shard_map(
        body,
        mesh=mesh,
        in_specs=(
            P(None, None, "lat", "lon"),
            P(None, None, "lat", "lon"),
            P(None, None, "lat", "lon"),
            P(("lat", "lon"), None, None, None),
            P(("lat", "lon"), None, None),
            P(("lat", "lon"), None),
        ),
        out_specs=P(None, None, "lat", "lon"),
        check_vma=False,
    )
```

```python
import functools

import jax
import jax.numpy as jnp
from jax import lax
from jax.experimental import pallas as pl
from jax.experimental.pallas import tpu as pltpu
from jax.sharding import PartitionSpec as P

DIFFUSION = 0.1
F32 = jnp.float32
BF16 = jnp.bfloat16

TARGET_ROW = 64
EDGE_ROW = 72
STRIP_ROW = 112
LON_ROWS = 192

A_AT, B_AT, C_AT, STRIP_AT = 16, 18, 19, 23
LAT_ROWS = 25 * 16
CENTRE = 1.0 - 4.0 * DIFFUSION


def pieces(values):
    high = values.astype(BF16)
    rest = values - high.astype(F32)
    middle = rest.astype(BF16)
    low = (rest - middle.astype(F32)).astype(BF16)
    return high, middle, low


def lanes_of(rows):
    return lax.broadcasted_iota(jnp.int32, (rows, 128), 1)


def levels(ref, field, row, first=0, count=16):
    return ref[field, pl.ds(first * 8 + row, count, stride=8), :]


def pack_blocks(tile, apart, count_ref, column_ref, values_ref, out_ref):
    slot = lax.broadcasted_iota(jnp.int32, (64, 128), 0)
    cell = lax.broadcasted_iota(jnp.int32, (64, 128), 0)
    side = cell >> 3
    wanted = (cell & 7) * 128 + jnp.where(side < 4, 124 + side, side - 4)
    lane = lanes_of(8)
    allowed = (lanes_of(64) < 64) == (side < 4)
    dest = tile ^ apart
    left, right = (dest + 3) & 3, (dest + 1) & 3
    block = lambda t: jnp.where(slot < count_ref[0, t], values_ref[t], 0.0)
    column = lambda t: column_ref[pl.ds(t, 1), :]
    out_ref[0:64, :] = block(dest)
    wide = jnp.concatenate([column(dest), jnp.zeros((1, 64), jnp.int32)], axis=1)
    out_ref[TARGET_ROW:EDGE_ROW, :] = jnp.broadcast_to(wide.astype(F32), (8, 128))
    target = jnp.concatenate([column(left), column(right)], axis=1)
    hit = jnp.where(jnp.logical_and(jnp.broadcast_to(target, (64, 128)) == wanted, allowed), 1.0, 0.0)
    hit = hit.astype(BF16)
    both = jnp.concatenate([block(left), block(right)], axis=0)
    total = jnp.zeros((64, 128), F32)
    for piece in pieces(both):
        total = total + jnp.dot(hit, piece, preferred_element_type=F32)
    at = [total[c * 8 : c * 8 + 8] for c in range(8)]
    for place, rows in enumerate(
        (
            at[3],
            at[4],
            jnp.where(lane < 32, pltpu.roll(at[0], 32, 1), at[2]),
            jnp.where(lane < 32, pltpu.roll(at[7], 32, 1), at[5]),
            jnp.where(lane < 64, pltpu.roll(at[6], 64, 1), at[1]),
        )
    ):
        out_ref[EDGE_ROW + place * 8 : EDGE_ROW + place * 8 + 8, :] = rows


def own_blocks_kernel(count_ref, column_ref, values_ref, out_ref):
    pack_blocks(lax.axis_index("lon"), 0, count_ref, column_ref, values_ref, out_ref)


def pack_kernel(*refs):
    sources, outs, copies_of, packed, strips_ref, sems = (
        refs[:6], refs[6:9], refs[9:15], refs[15:18], refs[18], refs[19]
    )
    copies = [pltpu.make_async_copy(sources[i], copies_of[i], sems.at[i]) for i in range(6)]
    for i in (2, 1, 0, 3, 5, 4):
        copies[i].start()
    for copy in copies[:3]:
        copy.wait()
    count_ref, column_ref, values_ref, lam_ref, winds_ref, coupling_ref = copies_of
    tile = lax.axis_index("lon")
    lane = lanes_of(8)
    sent = []
    for apart in (3, 2, 1):
        pack_blocks(tile, apart, count_ref, column_ref, values_ref, packed[apart - 1])
        sent.append(
            pltpu.make_async_copy(
                packed[apart - 1], outs[apart - 1].at[pl.ds(0, STRIP_ROW), :], sems.at[5 + apart]
            )
        )
        sent[-1].start()

    for copy in copies[3:]:
        copy.wait()
    row = 0
    for ref, fields in ((lam_ref, 4), (winds_ref, 2), (coupling_ref, 4)):
        for field in range(fields):
            strip = jnp.zeros((8, 128), F32)
            for half in range(2):
                for r in range(8):
                    at = half * 64 + r * 8
                    moved = pltpu.roll(levels(ref, field, r, half * 8, 8), (at + 4) % 128, 1)
                    strip = jnp.where(jnp.logical_and(lane >= at, lane < at + 8), moved, strip)
            strips_ref[row : row + 8, :] = strip
            row += 8
    for apart in (3, 1):
        sent.append(
            pltpu.make_async_copy(
                strips_ref, outs[apart - 1].at[pl.ds(STRIP_ROW, LON_ROWS - STRIP_ROW), :], sems.at[8 + apart]
            )
        )
        sent[-1].start()
    for copy in sent:
        copy.wait()


def strip_lane(plane, way):
    return ((plane % 16) * 8 + way * (88 if plane == A_AT + 1 else 72)) % 128


def once(make):
    made = {}

    def get(*key):
        if key not in made:
            made[key] = make(*key)
        return made[key]

    return get


def along(x, to_left, to_right, beside, at, lane):
    p_right, p_left = to_left * x, to_right * x
    edge = pltpu.roll(beside, (128 - (at + 4)) % 128, 1)
    right = jnp.where(lane == 127, edge, pltpu.roll(p_right, 127, 1))
    left = jnp.where(lane == 0, edge, pltpu.roll(p_left, 1, 1))
    return right + left, jnp.where(lane == 0, p_right, p_left)


def insert(inner, pair, at, lane):
    moved = pltpu.roll(pair, (at + 4) % 128, 1)
    return jnp.where(jnp.logical_or(lane == at + 4, lane == at + 3), moved, inner)


def strip_along(rolled_right, rolled_left, inner, side):
    right = jnp.where(side == 3, pltpu.roll(inner, 127, 1), rolled_right)
    left = jnp.where(side == 4, pltpu.roll(inner, 1, 1), rolled_left)
    return right + left


def own_steps(lam_ref, winds_ref, coupling_ref, force_ref, strips_ref, wanted, keep):
    lane = lanes_of(8)
    side = lane & 7
    strip_row = (lane >> 3) & 7

    def force(row, instant, field, half):
        at = instant * 32 + field * 16 + half * 8
        return force_ref[row, at : at + 8, :]

    half_wind = once(lambda axis, row, half: 0.5 * levels(winds_ref, axis, row, half * 8, 8))
    up_weight = once(lambda row, half: DIFFUSION + half_wind(0, row, half))
    down_weight = once(lambda row, half: DIFFUSION - half_wind(0, row, half))
    right_weight = once(lambda row, half: DIFFUSION + half_wind(1, row, half))
    left_weight = once(lambda row, half: DIFFUSION - half_wind(1, row, half))

    def strip(place):
        return strips_ref[place * 8 : place * 8 + 8, :]

    half_a, half_b = 0.5 * strip(4), 0.5 * strip(5)
    strip_up, strip_down = DIFFUSION + half_a, DIFFUSION - half_a
    strip_right, strip_left = DIFFUSION + half_b, DIFFUSION - half_b

    u = [{}, {}, {}, {}]
    for field in range(4):
        for half in range(2):
            for row in range(8):
                value = levels(lam_ref, field, row, half * 8, 8)
                if field >= 2:
                    value = value + force(row, 3, field - 2, half)
                u[field][row, half] = value
    strips = [strip(field) for field in range(4)]
    keep(0, u, strips)
    for step, rows in enumerate(wanted, 1):
        last = step == 4
        later = [{}, {}, {}, {}]
        later_strips = []
        for field in range(4):
            x = u[field]
            rolled_right = pltpu.roll(strip_right * strips[field], 127, 1)
            rolled_left = pltpu.roll(strip_left * strips[field], 1, 1)
            beside = jnp.where(side == 3, rolled_right, rolled_left)
            inner = beside
            for half in range(2):
                for row in rows:
                    at = half * 64 + row * 8
                    shares, pair = along(
                        x[row, half], right_weight(row, half), left_weight(row, half), beside, at, lane
                    )
                    total = CENTRE * x[row, half] + shares
                    if row < 7:
                        total = total + up_weight(row + 1, half) * x[row + 1, half]
                    if row > 0:
                        total = total + down_weight(row - 1, half) * x[row - 1, half]
                    if field < 2:
                        first = levels(coupling_ref, field, row, half * 8, 8)
                        second = levels(coupling_ref, field + 2, row, half * 8, 8)
                        total = total - (first * u[2][row, half] + second * u[3][row, half])
                    elif not last:
                        total = total + force(row, 3 - step, field - 2, half)
                    later[field][row, half] = total
                    if not last:
                        inner = insert(inner, pair, at, lane)
            if not last:
                total = CENTRE * strips[field] + strip_along(rolled_right, rolled_left, inner, side)
                total = total + jnp.where(strip_row == 7, 0.0, pltpu.roll(strip_up * strips[field], 120, 1))
                total = total + jnp.where(strip_row == 0, 0.0, pltpu.roll(strip_down * strips[field], 8, 1))
                if field < 2:
                    total = total - (strip(6 + field) * strips[2] + strip(8 + field) * strips[3])
                else:
                    total = total + strip(10 + 2 * (step - 1) + field - 2)
                later_strips.append(total)
        u, strips = later, later_strips
        keep(step, u, strips)


def halo_kernel(
    got3_ref, got2_ref, got1_ref, own_ref, lam_ref, winds_ref, coupling_ref, even_ref, odd_ref, force_ref, strips_ref, edge_ref
):
    is_even = lax.rem(lax.axis_index("lat"), 2) == 0
    right_is_1 = lax.rem(lax.axis_index("lon"), 2) == 0
    lane = lanes_of(8)
    lane1 = lanes_of(1)
    messages = (own_ref, got1_ref, got2_ref, got3_ref)

    rows = [message[TARGET_ROW : TARGET_ROW + 1, :] for message in messages]
    halves = [jnp.where(lane1 < 64, rows[s], pltpu.roll(rows[s + 1], 64, 1)) for s in (0, 2)]
    target = jnp.concatenate(halves, axis=1).astype(jnp.int32)
    blocks = jnp.concatenate([message[0:64, :] for message in messages], axis=0)
    stacked = jnp.concatenate(pieces(blocks.T), axis=0)
    cell = lax.broadcasted_iota(jnp.int32, (256, 256), 0)
    for pair in range(4):
        hit = jnp.where(jnp.broadcast_to(target, (256, 256)) == cell + pair * 256, 1.0, 0.0).astype(BF16)
        three = lax.dot_general(stacked, hit, (((1,), (1,)), ((), ())), preferred_element_type=F32)
        both = three[0:128] + three[128:256] + three[256:384]
        force_ref[2 * pair] = both[:, 0:128]
        force_ref[2 * pair + 1] = both[:, 128:256]

    near2, near1, far24, far42, thirds = [
        sum(message[EDGE_ROW + place * 8 : EDGE_ROW + place * 8 + 8, :] for message in messages)
        for place in (0, 1, 2, 3, 4)
    ]
    for c, rows in enumerate(
        (
            jnp.where(lane >= 96, pltpu.roll(far24, 96, 1), 0.0),
            jnp.where(lane >= 64, thirds, 0.0),
            jnp.where(lane >= 32, far24, 0.0),
            near2,
            near1,
            jnp.where(lane >= 32, far42, 0.0),
            jnp.where(lane >= 64, pltpu.roll(thirds, 64, 1), 0.0),
            jnp.where(lane >= 96, pltpu.roll(far42, 96, 1), 0.0),
        )
    ):
        edge_ref[pl.ds(c, 8, stride=8), :] = rows
        edge_ref[pl.ds(64 + c, 8, stride=8), :] = rows
    edge = edge_ref[...].T

    def edge_strip(instant, field):
        at = instant * 32 + field * 16
        return jnp.where(lane < 64, edge[at : at + 8], edge[at + 8 : at + 16])

    from_1 = ((lane & 7) < 4) != right_is_1
    for field in range(10):
        at = STRIP_ROW + field * 8
        strip = jnp.where(from_1, got1_ref[at : at + 8, :], got3_ref[at : at + 8, :])
        if field in (2, 3):
            strip = strip + edge_strip(3, field - 2)
        strips_ref[field * 8 : field * 8 + 8, :] = strip
    for place, (instant, field) in enumerate(((2, 0), (2, 1), (1, 0), (1, 1), (0, 0), (0, 1))):
        strips_ref[80 + place * 8 : 88 + place * 8, :] = edge_strip(instant, field)

    sides = {}

    def put(plane, half, up, down):
        at = plane * 16 + half * 8
        even_ref[at : at + 8, :] = jnp.where(is_even, up, down)
        odd_ref[at : at + 8, :] = jnp.where(is_even, down, up)

    def put_strip(plane, packed, up_row, down_row):
        for half in range(2):
            for way, row in ((0, up_row), (1, down_row)):
                at = strip_lane(plane, way)
                mine = jnp.logical_and(lane >= at, lane < at + 8)
                key = (STRIP_AT + plane // 16, half, way)
                moved = pltpu.roll(packed, (at - half * 64 - row * 8) % 128, 1)
                sides[key] = jnp.where(mine, moved, sides.get(key, 0.0))

    def keep(step, u, strips):
        for field in range(4):
            plane = step * 4 + field
            for half in range(2):
                put(plane, half, u[field][7, half], u[field][0, half])
            if step < 3:
                put_strip(plane, strips[field], 7, 0)

    own_steps(
        lam_ref,
        winds_ref,
        coupling_ref,
        force_ref,
        strips_ref,
        ((0, 1, 2, 5, 6, 7), (0, 1, 6, 7), (0, 7)),
        keep,
    )
    for plane, ref, field, depth in (
        (A_AT, winds_ref, 0, 0),
        (A_AT + 1, winds_ref, 0, 1),
        (B_AT, winds_ref, 1, 0),
        (C_AT, coupling_ref, 0, 0),
        (C_AT + 1, coupling_ref, 1, 0),
        (C_AT + 2, coupling_ref, 2, 0),
        (C_AT + 3, coupling_ref, 3, 0),
    ):
        for half in range(2):
            put(plane, half, levels(ref, field, 7 - depth, half * 8, 8), levels(ref, field, depth, half * 8, 8))
        place = field + (4 if ref is winds_ref else 6)
        put_strip(plane, strips_ref[place * 8 : place * 8 + 8, :], 7 - depth, depth)
    for plane in (STRIP_AT, STRIP_AT + 1):
        for half in range(2):
            put(plane, half, sides[plane, half, 0], sides[plane, half, 1])


def own_kernel(force_ref, strips_ref, lam_ref, winds_ref, coupling_ref, out_ref, wide_ref):
    every = tuple(range(8))

    def widen(place, packed):
        for half in range(2):
            at = (place * 2 + half) * 8
            wide_ref[at : at + 8, :] = pltpu.roll(packed, 16 if half == 0 else 80, 1)

    def keep(step, u, strips):
        for field in range(4):
            if step < 3:
                widen(step * 4 + field, strips[field])
            if step == 4:
                for half in range(2):
                    for row in range(8):
                        out_ref[field, row, half * 8 : half * 8 + 8, :] = u[field][row, half]

    for place in range(6):
        widen(12 + place, strips_ref[32 + place * 8 : 40 + place * 8, :])
    own_steps(lam_ref, winds_ref, coupling_ref, force_ref, strips_ref, (every,) * 4, keep)


def join_kernel(
    bands,
    odd_ref,
    even_ref,
    sent_odd_ref,
    sent_even_ref,
    own_ref,
    wide_ref,
    winds_ref,
    coupling_ref,
    out_ref,
    border_ref,
):
    band = lax.axis_index("lat")
    is_even = lax.rem(band, 2) == 0
    low_mask = jnp.where(band > 0, 1.0, 0.0).astype(F32)
    high_mask = jnp.where(band < bands - 1, 1.0, 0.0).astype(F32)
    lane = lanes_of(8)
    side = lane & 7
    strip_row = (lane >> 3) - 2
    strip_mask = jnp.where(strip_row < 0, low_mask, jnp.where(strip_row > 7, high_mask, 1.0))

    def chosen(first, second):
        def get(plane, half):
            at = plane * 16 + half * 8
            return jnp.where(is_even, first[at : at + 8, :], second[at : at + 8, :])

        return once(get)

    low, high = chosen(odd_ref, even_ref), chosen(even_ref, odd_ref)
    up, down = chosen(sent_even_ref, sent_odd_ref), chosen(sent_odd_ref, sent_even_ref)
    border_of = {-1: low, 0: down, 7: up, 8: high}

    def outer(first, row, half, own):
        if row < 0:
            return low(first - 1 - row, half)
        if row > 7:
            return high(first + row - 8, half)
        return own

    def half_wind(axis, row, half):
        own = levels(winds_ref, axis, row, half * 8, 8) if 0 <= row <= 7 else None
        return 0.5 * outer(A_AT if axis == 0 else B_AT, row, half, own)

    half_wind = once(half_wind)
    up_weight = once(lambda row, half: DIFFUSION + half_wind(0, row, half))
    down_weight = once(lambda row, half: DIFFUSION - half_wind(0, row, half))
    right_weight = once(lambda row, half: DIFFUSION + half_wind(1, row, half))
    left_weight = once(lambda row, half: DIFFUSION - half_wind(1, row, half))

    def couple(field, row, half):
        own = levels(coupling_ref, field, row, half * 8, 8) if 0 <= row <= 7 else None
        return outer(C_AT + field, row, half, own)

    couple = once(couple)

    def met(plane, half):
        at = strip_lane(plane, 0)
        mine = jnp.logical_and(lane >= at, lane < at + 8)
        both = jnp.where(mine, low(STRIP_AT + plane // 16, half), high(STRIP_AT + plane // 16, half))
        return pltpu.roll(both, ((0 if plane == A_AT + 1 else 8) - at) % 128, 1)

    inside = jnp.logical_and(strip_row >= 0, strip_row <= 7)

    def strip(place, plane, half):
        at = (place * 2 + half) * 8
        return jnp.where(inside, wide_ref[at : at + 8, :], met(plane, half))

    for plane in range(12):
        for half in range(2):
            at = (plane * 2 + half) * 8
            border_ref[at : at + 8, :] = strip(plane, plane, half)
    deepest = jnp.logical_or(strip_row == -2, strip_row == 9)
    strip_a = [
        0.5 * jnp.where(deepest, met(A_AT + 1, half), strip(12, A_AT, half)) for half in range(2)
    ]
    strip_b = [0.5 * strip(13, B_AT, half) for half in range(2)]
    strip_c = [[strip(14 + field, C_AT + field, half) for half in range(2)] for field in range(4)]

    e = [{}, {}, {}, {}]
    strips = [[None, None] for _ in range(4)]
    reach = ((-1, 0), (-2, -1, 0, 1), (-1, 0, 1, 2), (0, 1, 2, 3))
    for step in range(4):
        last = step == 3
        rows = reach[step] + tuple(7 - row for row in reach[step])
        later = [{}, {}, {}, {}]
        later_strips = [[None, None] for _ in range(4)]
        for field in range(4):
            x = e[field]
            plane = step * 4 + field
            for half in range(2):
                xs = strips[field][half]
                if step > 0:
                    rolled_right = pltpu.roll((DIFFUSION + strip_b[half]) * xs, 127, 1)
                    rolled_left = pltpu.roll((DIFFUSION - strip_b[half]) * xs, 1, 1)
                    beside = jnp.where(side == 3, rolled_right, rolled_left)
                    inner = beside
                for row in rows:
                    terms = []
                    if (row, half) in x:
                        here = x[row, half]
                        at = (row + 2) * 8
                        shares, pair = along(
                            here, right_weight(row, half), left_weight(row, half), beside, at, lane
                        )
                        local = CENTRE * here + shares
                        if field < 2:
                            local = local - (
                                couple(field, row, half) * e[2][row, half]
                                + couple(field + 2, row, half) * e[3][row, half]
                            )
                        terms.append(local)
                        if not last:
                            inner = insert(inner, pair, at, lane)
                    for near, crossing, weight in (
                        (row + 1, (0, 8), up_weight),
                        (row - 1, (-1, 7), down_weight),
                    ):
                        parts = []
                        if (near, half) in x:
                            parts.append(x[near, half])
                        if near in crossing:
                            parts.append(border_of[near](plane, half))
                        if parts:
                            terms.append(weight(near, half) * sum(parts[1:], parts[0]))
                    total = sum(terms[1:], terms[0])
                    if row == -1:
                        total = total * low_mask
                    if row == 8:
                        total = total * high_mask
                    if last:
                        total = total + own_ref[field, row, half * 8 : half * 8 + 8, :]
                        out_ref[field, pl.ds(half * 64 + row, 8, stride=8), :] = total
                    else:
                        later[field][row, half] = total
                if not last:
                    at = (plane * 2 + half) * 8
                    border = border_ref[at : at + 8, :]
                    from_above = jnp.where(jnp.logical_or(strip_row == 0, strip_row == 8), border, 0.0)
                    from_below = jnp.where(jnp.logical_or(strip_row == -1, strip_row == 7), border, 0.0)
                    if step > 0:
                        from_above, from_below = from_above + xs, from_below + xs
                    total = pltpu.roll((DIFFUSION + strip_a[half]) * from_above, 120, 1)
                    total = total + pltpu.roll((DIFFUSION - strip_a[half]) * from_below, 8, 1)
                    if step > 0:
                        total = total + CENTRE * xs + strip_along(rolled_right, rolled_left, inner, side)
                        if field < 2:
                            total = total - (
                                strip_c[field][half] * strips[2][half] + strip_c[field + 2][half] * strips[3][half]
                            )
                    later_strips[field][half] = total * strip_mask
        e, strips = later, later_strips


def vmem(count):
    return [pl.BlockSpec(memory_space=pltpu.VMEM)] * count


def params(mebibytes=24):
    return pltpu.CompilerParams(vmem_limit_bytes=mebibytes * 1024 * 1024)


def body(lam_end, winds, coupling, obs_values, obs_column, obs_count):
    bands = lax.axis_size("lat")
    tiles = lax.axis_size("lon")
    lam = lam_end.reshape(4, 128, 128)
    wind = winds.reshape(2, 128, 128)
    couple = coupling.reshape(4, 128, 128)

    lon_rows = (LON_ROWS, STRIP_ROW, LON_ROWS)
    parts = pl.pallas_call(
        pack_kernel,
        out_shape=tuple(jax.ShapeDtypeStruct((rows, 128), F32) for rows in lon_rows),
        in_specs=[pl.BlockSpec(memory_space=pltpu.HBM)] * 6,
        out_specs=tuple([pl.BlockSpec(memory_space=pltpu.HBM)] * 3),
        scratch_shapes=[
            pltpu.SMEM((1, 4), jnp.int32),
            pltpu.VMEM((4, 64), jnp.int32),
            pltpu.VMEM((4, 64, 128), F32),
            pltpu.VMEM((4, 128, 128), F32),
            pltpu.VMEM((2, 128, 128), F32),
            pltpu.VMEM((4, 128, 128), F32),
            pltpu.VMEM((STRIP_ROW, 128), F32),
            pltpu.VMEM((STRIP_ROW, 128), F32),
            pltpu.VMEM((STRIP_ROW, 128), F32),
            pltpu.VMEM((LON_ROWS - STRIP_ROW, 128), F32),
            pltpu.SemaphoreType.DMA((12,)),
        ],
        compiler_params=params(60),
        name="pack_blocks_and_strips",
    )(obs_count, obs_column[0], obs_values[0], lam, wind, couple)
    got3, got2, got1 = [
        lax.ppermute(parts[apart - 1], "lon", [(i, i ^ apart) for i in range(tiles)]) for apart in (3, 2, 1)
    ]

    own_part = pl.pallas_call(
        own_blocks_kernel,
        out_shape=jax.ShapeDtypeStruct((STRIP_ROW, 128), F32),
        in_specs=[pl.BlockSpec(memory_space=pltpu.SMEM)] + vmem(2),
        out_specs=vmem(1)[0],
        compiler_params=params(),
        cost_estimate=pl.CostEstimate(flops=5_000_000, bytes_accessed=1_000_000, transcendentals=0),
        name="own_blocks",
    )(obs_count, obs_column[0], obs_values[0])

    halo = jax.ShapeDtypeStruct((LAT_ROWS, 128), F32)
    even, odd, force, strips = pl.pallas_call(
        halo_kernel,
        out_shape=(
            halo,
            halo,
            jax.ShapeDtypeStruct((8, 128, 128), F32),
            jax.ShapeDtypeStruct((128, 128), F32),
        ),
        in_specs=vmem(7),
        out_specs=tuple(vmem(4)),
        scratch_shapes=[pltpu.VMEM((128, 128), F32)],
        compiler_params=params(),
        name="scatter_and_halo",
    )(got3, got2, got1, own_part, lam, wind, couple)
    swap = lambda first: [p for i in range(first, bands - 1, 2) for p in ((i, i + 1), (i + 1, i))]
    got_odd = lax.ppermute(odd, "lat", swap(1))
    got_even = lax.ppermute(even, "lat", swap(0))

    own, wide = pl.pallas_call(
        own_kernel,
        out_shape=(jax.ShapeDtypeStruct((4, 8, 16, 128), F32), jax.ShapeDtypeStruct((288, 128), F32)),
        in_specs=vmem(5),
        out_specs=tuple(vmem(2)),
        compiler_params=params(),
        cost_estimate=pl.CostEstimate(flops=10_000_000, bytes_accessed=2_000_000, transcendentals=0),
        name="own_steps",
    )(force, strips, lam, wind, couple)

    out = pl.pallas_call(
        functools.partial(join_kernel, bands),
        out_shape=jax.ShapeDtypeStruct((4, 128, 128), F32),
        in_specs=vmem(8),
        out_specs=vmem(1)[0],
        scratch_shapes=[pltpu.VMEM((192, 128), F32)],
        compiler_params=params(),
        name="join_bands",
    )(got_odd, got_even, odd, even, own, wide, wind, couple)
    return out.reshape(lam_end.shape)


def solution(mesh):
    return jax.shard_map(
        body,
        mesh=mesh,
        in_specs=(
            P(None, None, "lat", "lon"),
            P(None, None, "lat", "lon"),
            P(None, None, "lat", "lon"),
            P(("lat", "lon"), None, None, None),
            P(("lat", "lon"), None, None),
            P(("lat", "lon"), None),
        ),
        out_specs=P(None, None, "lat", "lon"),
        check_vma=False,
    )
```

```python
import functools

import jax
import jax.numpy as jnp
from jax import lax
from jax.experimental import pallas as pl
from jax.experimental.pallas import tpu as pltpu
from jax.sharding import PartitionSpec as P

DIFFUSION = 0.1
F32 = jnp.float32
BF16 = jnp.bfloat16

TARGET_ROW = 64
EDGE_ROW = 72
STRIP_ROW = 112
LON_ROWS = 192

A_AT, B_AT, C_AT, STRIP_AT = 16, 18, 19, 23
LAT_ROWS = 25 * 16
CENTRE = 1.0 - 4.0 * DIFFUSION


def pieces(values):
    high = values.astype(BF16)
    rest = values - high.astype(F32)
    middle = rest.astype(BF16)
    low = (rest - middle.astype(F32)).astype(BF16)
    return high, middle, low


def lanes_of(rows):
    return lax.broadcasted_iota(jnp.int32, (rows, 128), 1)


def levels(ref, field, row, first=0, count=16):
    return ref[field, pl.ds(first * 8 + row, count, stride=8), :]


def pack_blocks(tile, apart, count_ref, column_ref, values_ref, out_ref):
    slot = lax.broadcasted_iota(jnp.int32, (64, 128), 0)
    cell = lax.broadcasted_iota(jnp.int32, (64, 128), 0)
    side = cell >> 3
    wanted = (cell & 7) * 128 + jnp.where(side < 4, 124 + side, side - 4)
    lane = lanes_of(8)
    allowed = (lanes_of(64) < 64) == (side < 4)
    dest = tile ^ apart
    left, right = (dest + 3) & 3, (dest + 1) & 3
    block = lambda t: jnp.where(slot < count_ref[0, t], values_ref[t], 0.0)
    column = lambda t: column_ref[pl.ds(t, 1), :]
    out_ref[0:64, :] = block(dest)
    wide = jnp.concatenate([column(dest), jnp.zeros((1, 64), jnp.int32)], axis=1)
    out_ref[TARGET_ROW:EDGE_ROW, :] = jnp.broadcast_to(wide.astype(F32), (8, 128))
    target = jnp.concatenate([column(left), column(right)], axis=1)
    hit = jnp.where(jnp.logical_and(jnp.broadcast_to(target, (64, 128)) == wanted, allowed), 1.0, 0.0)
    hit = hit.astype(BF16)
    both = jnp.concatenate([block(left), block(right)], axis=0)
    total = jnp.zeros((64, 128), F32)
    for piece in pieces(both):
        total = total + jnp.dot(hit, piece, preferred_element_type=F32)
    at = [total[c * 8 : c * 8 + 8] for c in range(8)]
    for place, rows in enumerate(
        (
            at[3],
            at[4],
            jnp.where(lane < 32, pltpu.roll(at[0], 32, 1), at[2]),
            jnp.where(lane < 32, pltpu.roll(at[7], 32, 1), at[5]),
            jnp.where(lane < 64, pltpu.roll(at[6], 64, 1), at[1]),
        )
    ):
        out_ref[EDGE_ROW + place * 8 : EDGE_ROW + place * 8 + 8, :] = rows


def own_blocks_kernel(count_ref, column_ref, values_ref, out_ref):
    pack_blocks(lax.axis_index("lon"), 0, count_ref, column_ref, values_ref, out_ref)


def pack_kernel(*refs):
    sources, outs, copies_of, sems = refs[:6], refs[6:9], refs[9:15], refs[15]
    copies = [pltpu.make_async_copy(sources[i], copies_of[i], sems.at[i]) for i in range(6)]
    for i in (2, 1, 0, 3, 5, 4):
        copies[i].start()
    for copy in copies[:3]:
        copy.wait()
    count_ref, column_ref, values_ref, lam_ref, winds_ref, coupling_ref = copies_of
    tile = lax.axis_index("lon")
    lane = lanes_of(8)
    for apart in (3, 2, 1):
        pack_blocks(tile, apart, count_ref, column_ref, values_ref, outs[apart - 1])

    for copy in copies[3:]:
        copy.wait()
    row = STRIP_ROW
    for ref, fields in ((lam_ref, 4), (winds_ref, 2), (coupling_ref, 4)):
        for field in range(fields):
            strip = jnp.zeros((8, 128), F32)
            for half in range(2):
                for r in range(8):
                    at = half * 64 + r * 8
                    moved = pltpu.roll(levels(ref, field, r, half * 8, 8), (at + 4) % 128, 1)
                    strip = jnp.where(jnp.logical_and(lane >= at, lane < at + 8), moved, strip)
            for apart in (1, 3):
                outs[apart - 1][row : row + 8, :] = strip
            row += 8


def strip_lane(plane, way):
    return ((plane % 16) * 8 + way * (88 if plane == A_AT + 1 else 72)) % 128


def once(make):
    made = {}

    def get(*key):
        if key not in made:
            made[key] = make(*key)
        return made[key]

    return get


def along(x, to_left, to_right, beside, at, lane):
    p_right, p_left = to_left * x, to_right * x
    strip_right, strip_left = beside
    right = jnp.where(lane == 127, pltpu.roll(strip_right, (123 - at) % 128, 1), pltpu.roll(p_right, 127, 1))
    left = jnp.where(lane == 0, pltpu.roll(strip_left, (125 - at) % 128, 1), pltpu.roll(p_left, 1, 1))
    return right + left, (p_right, p_left)


def insert(inner, pair, at, lane):
    p_right, p_left = pair
    inner = jnp.where(lane == at + 3, pltpu.roll(p_right, (at + 3) % 128, 1), inner)
    return jnp.where(lane == at + 4, pltpu.roll(p_left, (at + 5) % 128, 1), inner)


def strip_along(rolled_right, rolled_left, inner, side):
    right = jnp.where(side == 3, inner, rolled_right)
    left = jnp.where(side == 4, inner, rolled_left)
    return right + left


def own_steps(lam_ref, winds_ref, coupling_ref, force_ref, strips_ref, wanted, keep):
    lane = lanes_of(8)
    side = lane & 7
    strip_row = (lane >> 3) & 7

    def force(row, instant, field, half):
        at = instant * 32 + field * 16 + half * 8
        return force_ref[row, at : at + 8, :]

    half_wind = once(lambda axis, row, half: 0.5 * levels(winds_ref, axis, row, half * 8, 8))
    up_weight = once(lambda row, half: DIFFUSION + half_wind(0, row, half))
    down_weight = once(lambda row, half: DIFFUSION - half_wind(0, row, half))
    right_weight = once(lambda row, half: DIFFUSION + half_wind(1, row, half))
    left_weight = once(lambda row, half: DIFFUSION - half_wind(1, row, half))

    def strip(place):
        return strips_ref[place * 8 : place * 8 + 8, :]

    half_a, half_b = 0.5 * strip(4), 0.5 * strip(5)
    strip_up, strip_down = DIFFUSION + half_a, DIFFUSION - half_a
    strip_right, strip_left = DIFFUSION + half_b, DIFFUSION - half_b

    u = [{}, {}, {}, {}]
    for field in range(4):
        for half in range(2):
            for row in range(8):
                value = levels(lam_ref, field, row, half * 8, 8)
                if field >= 2:
                    value = value + force(row, 3, field - 2, half)
                u[field][row, half] = value
    strips = [strip(field) for field in range(4)]
    keep(0, u, strips)
    for step, rows in enumerate(wanted, 1):
        last = step == 4
        later = [{}, {}, {}, {}]
        later_strips = []
        for field in range(4):
            x = u[field]
            beside = (strip_right * strips[field], strip_left * strips[field])
            rolled_right = pltpu.roll(beside[0], 127, 1)
            rolled_left = pltpu.roll(beside[1], 1, 1)
            inner = beside[0]
            for half in range(2):
                for row in rows:
                    at = half * 64 + row * 8
                    shares, pair = along(
                        x[row, half], right_weight(row, half), left_weight(row, half), beside, at, lane
                    )
                    total = CENTRE * x[row, half] + shares
                    if row < 7:
                        total = total + up_weight(row + 1, half) * x[row + 1, half]
                    if row > 0:
                        total = total + down_weight(row - 1, half) * x[row - 1, half]
                    if field < 2:
                        first = levels(coupling_ref, field, row, half * 8, 8)
                        second = levels(coupling_ref, field + 2, row, half * 8, 8)
                        total = total - (first * u[2][row, half] + second * u[3][row, half])
                    elif not last:
                        total = total + force(row, 3 - step, field - 2, half)
                    later[field][row, half] = total
                    if not last:
                        inner = insert(inner, pair, at, lane)
            if not last:
                total = CENTRE * strips[field] + strip_along(rolled_right, rolled_left, inner, side)
                total = total + jnp.where(strip_row == 7, 0.0, pltpu.roll(strip_up * strips[field], 120, 1))
                total = total + jnp.where(strip_row == 0, 0.0, pltpu.roll(strip_down * strips[field], 8, 1))
                if field < 2:
                    total = total - (strip(6 + field) * strips[2] + strip(8 + field) * strips[3])
                else:
                    total = total + strip(10 + 2 * (step - 1) + field - 2)
                later_strips.append(total)
        u, strips = later, later_strips
        keep(step, u, strips)


def halo_kernel(
    got3_ref, got2_ref, got1_ref, own_ref, lam_ref, winds_ref, coupling_ref, even_ref, odd_ref, force_ref, strips_ref, edge_ref
):
    is_even = lax.rem(lax.axis_index("lat"), 2) == 0
    right_is_1 = lax.rem(lax.axis_index("lon"), 2) == 0
    lane = lanes_of(8)
    lane1 = lanes_of(1)
    messages = (own_ref, got1_ref, got2_ref, got3_ref)

    rows = [message[TARGET_ROW : TARGET_ROW + 1, :] for message in messages]
    halves = [jnp.where(lane1 < 64, rows[s], pltpu.roll(rows[s + 1], 64, 1)) for s in (0, 2)]
    target = jnp.concatenate(halves, axis=1).astype(jnp.int32)
    blocks = jnp.concatenate([message[0:64, :] for message in messages], axis=0)
    stacked = jnp.concatenate(pieces(blocks.T), axis=0)
    cell = lax.broadcasted_iota(jnp.int32, (256, 256), 0)
    for pair in range(4):
        hit = jnp.where(jnp.broadcast_to(target, (256, 256)) == cell + pair * 256, 1.0, 0.0).astype(BF16)
        three = lax.dot_general(stacked, hit, (((1,), (1,)), ((), ())), preferred_element_type=F32)
        both = three[0:128] + three[128:256] + three[256:384]
        force_ref[2 * pair] = both[:, 0:128]
        force_ref[2 * pair + 1] = both[:, 128:256]

    near2, near1, far24, far42, thirds = [
        sum(message[EDGE_ROW + place * 8 : EDGE_ROW + place * 8 + 8, :] for message in messages)
        for place in (0, 1, 2, 3, 4)
    ]
    for c, rows in enumerate(
        (
            jnp.where(lane >= 96, pltpu.roll(far24, 96, 1), 0.0),
            jnp.where(lane >= 64, thirds, 0.0),
            jnp.where(lane >= 32, far24, 0.0),
            near2,
            near1,
            jnp.where(lane >= 32, far42, 0.0),
            jnp.where(lane >= 64, pltpu.roll(thirds, 64, 1), 0.0),
            jnp.where(lane >= 96, pltpu.roll(far42, 96, 1), 0.0),
        )
    ):
        edge_ref[pl.ds(c, 8, stride=8), :] = rows
        edge_ref[pl.ds(64 + c, 8, stride=8), :] = rows
    edge = edge_ref[...].T

    def edge_strip(instant, field):
        at = instant * 32 + field * 16
        return jnp.where(lane < 64, edge[at : at + 8], edge[at + 8 : at + 16])

    from_1 = ((lane & 7) < 4) != right_is_1
    for field in range(10):
        at = STRIP_ROW + field * 8
        strip = jnp.where(from_1, got1_ref[at : at + 8, :], got3_ref[at : at + 8, :])
        if field in (2, 3):
            strip = strip + edge_strip(3, field - 2)
        strips_ref[field * 8 : field * 8 + 8, :] = strip
    for place, (instant, field) in enumerate(((2, 0), (2, 1), (1, 0), (1, 1), (0, 0), (0, 1))):
        strips_ref[80 + place * 8 : 88 + place * 8, :] = edge_strip(instant, field)

    sides = {}

    def put(plane, half, up, down):
        at = plane * 16 + half * 8
        even_ref[at : at + 8, :] = jnp.where(is_even, up, down)
        odd_ref[at : at + 8, :] = jnp.where(is_even, down, up)

    def put_strip(plane, packed, up_row, down_row):
        for half in range(2):
            for way, row in ((0, up_row), (1, down_row)):
                at = strip_lane(plane, way)
                mine = jnp.logical_and(lane >= at, lane < at + 8)
                key = (STRIP_AT + plane // 16, half, way)
                moved = pltpu.roll(packed, (at - half * 64 - row * 8) % 128, 1)
                sides[key] = jnp.where(mine, moved, sides.get(key, 0.0))

    def keep(step, u, strips):
        for field in range(4):
            plane = step * 4 + field
            for half in range(2):
                put(plane, half, u[field][7, half], u[field][0, half])
            if step < 3:
                put_strip(plane, strips[field], 7, 0)

    own_steps(
        lam_ref,
        winds_ref,
        coupling_ref,
        force_ref,
        strips_ref,
        ((0, 1, 2, 5, 6, 7), (0, 1, 6, 7), (0, 7)),
        keep,
    )
    for plane, ref, field, depth in (
        (A_AT, winds_ref, 0, 0),
        (A_AT + 1, winds_ref, 0, 1),
        (B_AT, winds_ref, 1, 0),
        (C_AT, coupling_ref, 0, 0),
        (C_AT + 1, coupling_ref, 1, 0),
        (C_AT + 2, coupling_ref, 2, 0),
        (C_AT + 3, coupling_ref, 3, 0),
    ):
        for half in range(2):
            put(plane, half, levels(ref, field, 7 - depth, half * 8, 8), levels(ref, field, depth, half * 8, 8))
        place = field + (4 if ref is winds_ref else 6)
        put_strip(plane, strips_ref[place * 8 : place * 8 + 8, :], 7 - depth, depth)
    for plane in (STRIP_AT, STRIP_AT + 1):
        for half in range(2):
            put(plane, half, sides[plane, half, 0], sides[plane, half, 1])


def own_kernel(force_ref, strips_ref, lam_ref, winds_ref, coupling_ref, out_ref, wide_ref):
    every = tuple(range(8))

    def widen(place, packed):
        for half in range(2):
            at = (place * 2 + half) * 8
            wide_ref[at : at + 8, :] = pltpu.roll(packed, 16 if half == 0 else 80, 1)

    def keep(step, u, strips):
        for field in range(4):
            if step < 3:
                widen(step * 4 + field, strips[field])
            if step == 4:
                for half in range(2):
                    for row in range(8):
                        out_ref[field, row, half * 8 : half * 8 + 8, :] = u[field][row, half]

    for place in range(6):
        widen(12 + place, strips_ref[32 + place * 8 : 40 + place * 8, :])
    own_steps(lam_ref, winds_ref, coupling_ref, force_ref, strips_ref, (every,) * 4, keep)


def join_kernel(
    bands,
    odd_ref,
    even_ref,
    sent_odd_ref,
    sent_even_ref,
    own_ref,
    wide_ref,
    winds_ref,
    coupling_ref,
    out_ref,
    border_ref,
):
    band = lax.axis_index("lat")
    is_even = lax.rem(band, 2) == 0
    low_mask = jnp.where(band > 0, 1.0, 0.0).astype(F32)
    high_mask = jnp.where(band < bands - 1, 1.0, 0.0).astype(F32)
    lane = lanes_of(8)
    side = lane & 7
    strip_row = (lane >> 3) - 2
    strip_mask = jnp.where(strip_row < 0, low_mask, jnp.where(strip_row > 7, high_mask, 1.0))

    def chosen(first, second):
        def get(plane, half):
            at = plane * 16 + half * 8
            return jnp.where(is_even, first[at : at + 8, :], second[at : at + 8, :])

        return once(get)

    low, high = chosen(odd_ref, even_ref), chosen(even_ref, odd_ref)
    up, down = chosen(sent_even_ref, sent_odd_ref), chosen(sent_odd_ref, sent_even_ref)
    border_of = {-1: low, 0: down, 7: up, 8: high}

    def outer(first, row, half, own):
        if row < 0:
            return low(first - 1 - row, half)
        if row > 7:
            return high(first + row - 8, half)
        return own

    def half_wind(axis, row, half):
        own = levels(winds_ref, axis, row, half * 8, 8) if 0 <= row <= 7 else None
        return 0.5 * outer(A_AT if axis == 0 else B_AT, row, half, own)

    half_wind = once(half_wind)
    up_weight = once(lambda row, half: DIFFUSION + half_wind(0, row, half))
    down_weight = once(lambda row, half: DIFFUSION - half_wind(0, row, half))
    right_weight = once(lambda row, half: DIFFUSION + half_wind(1, row, half))
    left_weight = once(lambda row, half: DIFFUSION - half_wind(1, row, half))

    def couple(field, row, half):
        own = levels(coupling_ref, field, row, half * 8, 8) if 0 <= row <= 7 else None
        return outer(C_AT + field, row, half, own)

    couple = once(couple)

    def met(plane, half):
        at = strip_lane(plane, 0)
        mine = jnp.logical_and(lane >= at, lane < at + 8)
        both = jnp.where(mine, low(STRIP_AT + plane // 16, half), high(STRIP_AT + plane // 16, half))
        return pltpu.roll(both, ((0 if plane == A_AT + 1 else 8) - at) % 128, 1)

    inside = jnp.logical_and(strip_row >= 0, strip_row <= 7)

    def strip(place, plane, half):
        at = (place * 2 + half) * 8
        return jnp.where(inside, wide_ref[at : at + 8, :], met(plane, half))

    for plane in range(12):
        for half in range(2):
            at = (plane * 2 + half) * 8
            border_ref[at : at + 8, :] = strip(plane, plane, half)
    deepest = jnp.logical_or(strip_row == -2, strip_row == 9)
    strip_a = [
        0.5 * jnp.where(deepest, met(A_AT + 1, half), strip(12, A_AT, half)) for half in range(2)
    ]
    strip_b = [0.5 * strip(13, B_AT, half) for half in range(2)]
    strip_c = [[strip(14 + field, C_AT + field, half) for half in range(2)] for field in range(4)]

    e = [{}, {}, {}, {}]
    strips = [[None, None] for _ in range(4)]
    reach = ((-1, 0), (-2, -1, 0, 1), (-1, 0, 1, 2), (0, 1, 2, 3))
    for step in range(4):
        last = step == 3
        rows = reach[step] + tuple(7 - row for row in reach[step])
        later = [{}, {}, {}, {}]
        later_strips = [[None, None] for _ in range(4)]
        for field in range(4):
            x = e[field]
            plane = step * 4 + field
            for half in range(2):
                xs = strips[field][half]
                if step > 0:
                    beside = ((DIFFUSION + strip_b[half]) * xs, (DIFFUSION - strip_b[half]) * xs)
                    rolled_right = pltpu.roll(beside[0], 127, 1)
                    rolled_left = pltpu.roll(beside[1], 1, 1)
                    inner = beside[0]
                for row in rows:
                    terms = []
                    if (row, half) in x:
                        here = x[row, half]
                        at = (row + 2) * 8
                        shares, pair = along(
                            here, right_weight(row, half), left_weight(row, half), beside, at, lane
                        )
                        local = CENTRE * here + shares
                        if field < 2:
                            local = local - (
                                couple(field, row, half) * e[2][row, half]
                                + couple(field + 2, row, half) * e[3][row, half]
                            )
                        terms.append(local)
                        if not last:
                            inner = insert(inner, pair, at, lane)
                    for near, crossing, weight in (
                        (row + 1, (0, 8), up_weight),
                        (row - 1, (-1, 7), down_weight),
                    ):
                        parts = []
                        if (near, half) in x:
                            parts.append(x[near, half])
                        if near in crossing:
                            parts.append(border_of[near](plane, half))
                        if parts:
                            terms.append(weight(near, half) * sum(parts[1:], parts[0]))
                    total = sum(terms[1:], terms[0])
                    if row == -1:
                        total = total * low_mask
                    if row == 8:
                        total = total * high_mask
                    if last:
                        total = total + own_ref[field, row, half * 8 : half * 8 + 8, :]
                        out_ref[field, pl.ds(half * 64 + row, 8, stride=8), :] = total
                    else:
                        later[field][row, half] = total
                if not last:
                    at = (plane * 2 + half) * 8
                    border = border_ref[at : at + 8, :]
                    from_above = jnp.where(jnp.logical_or(strip_row == 0, strip_row == 8), border, 0.0)
                    from_below = jnp.where(jnp.logical_or(strip_row == -1, strip_row == 7), border, 0.0)
                    if step > 0:
                        from_above, from_below = from_above + xs, from_below + xs
                    total = pltpu.roll((DIFFUSION + strip_a[half]) * from_above, 120, 1)
                    total = total + pltpu.roll((DIFFUSION - strip_a[half]) * from_below, 8, 1)
                    if step > 0:
                        total = total + CENTRE * xs + strip_along(rolled_right, rolled_left, inner, side)
                        if field < 2:
                            total = total - (
                                strip_c[field][half] * strips[2][half] + strip_c[field + 2][half] * strips[3][half]
                            )
                    later_strips[field][half] = total * strip_mask
        e, strips = later, later_strips


def vmem(count):
    return [pl.BlockSpec(memory_space=pltpu.VMEM)] * count


def params(mebibytes=24):
    return pltpu.CompilerParams(vmem_limit_bytes=mebibytes * 1024 * 1024)


def body(lam_end, winds, coupling, obs_values, obs_column, obs_count):
    bands = lax.axis_size("lat")
    tiles = lax.axis_size("lon")
    lam = lam_end.reshape(4, 128, 128)
    wind = winds.reshape(2, 128, 128)
    couple = coupling.reshape(4, 128, 128)

    lon_rows = (LON_ROWS, STRIP_ROW, LON_ROWS)
    parts = pl.pallas_call(
        pack_kernel,
        out_shape=tuple(jax.ShapeDtypeStruct((rows, 128), F32) for rows in lon_rows),
        in_specs=[pl.BlockSpec(memory_space=pltpu.HBM)] * 6,
        out_specs=tuple(vmem(3)),
        scratch_shapes=[
            pltpu.SMEM((1, 4), jnp.int32),
            pltpu.VMEM((4, 64), jnp.int32),
            pltpu.VMEM((4, 64, 128), F32),
            pltpu.VMEM((4, 128, 128), F32),
            pltpu.VMEM((2, 128, 128), F32),
            pltpu.VMEM((4, 128, 128), F32),
            pltpu.SemaphoreType.DMA((6,)),
        ],
        compiler_params=pltpu.CompilerParams(vmem_limit_bytes=54950 * 1024),
        name="pack_blocks_and_strips",
    )(obs_count, obs_column[0], obs_values[0], lam, wind, couple)
    got3, got2, got1 = [
        lax.ppermute(parts[apart - 1], "lon", [(i, i ^ apart) for i in range(tiles)]) for apart in (3, 2, 1)
    ]

    own_part = pl.pallas_call(
        own_blocks_kernel,
        out_shape=jax.ShapeDtypeStruct((STRIP_ROW, 128), F32),
        in_specs=[pl.BlockSpec(memory_space=pltpu.SMEM)] + vmem(2),
        out_specs=vmem(1)[0],
        compiler_params=params(),
        cost_estimate=pl.CostEstimate(flops=5_000_000, bytes_accessed=1_000_000, transcendentals=0),
        name="own_blocks",
    )(obs_count, obs_column[0], obs_values[0])

    halo = jax.ShapeDtypeStruct((LAT_ROWS, 128), F32)
    even, odd, force, strips = pl.pallas_call(
        halo_kernel,
        out_shape=(
            halo,
            halo,
            jax.ShapeDtypeStruct((8, 128, 128), F32),
            jax.ShapeDtypeStruct((128, 128), F32),
        ),
        in_specs=vmem(7),
        out_specs=tuple(vmem(4)),
        scratch_shapes=[pltpu.VMEM((128, 128), F32)],
        compiler_params=params(),
        name="scatter_and_halo",
    )(got3, got2, got1, own_part, lam, wind, couple)
    swap = lambda first: [p for i in range(first, bands - 1, 2) for p in ((i, i + 1), (i + 1, i))]
    got_odd = lax.ppermute(odd, "lat", swap(1))
    got_even = lax.ppermute(even, "lat", swap(0))

    own, wide = pl.pallas_call(
        own_kernel,
        out_shape=(jax.ShapeDtypeStruct((4, 8, 16, 128), F32), jax.ShapeDtypeStruct((288, 128), F32)),
        in_specs=vmem(5),
        out_specs=tuple(vmem(2)),
        compiler_params=params(),
        cost_estimate=pl.CostEstimate(flops=10_000_000, bytes_accessed=2_000_000, transcendentals=0),
        name="own_steps",
    )(force, strips, lam, wind, couple)

    out = pl.pallas_call(
        functools.partial(join_kernel, bands),
        out_shape=jax.ShapeDtypeStruct((4, 128, 128), F32),
        in_specs=vmem(8),
        out_specs=vmem(1)[0],
        scratch_shapes=[pltpu.VMEM((192, 128), F32)],
        compiler_params=params(),
        name="join_bands",
    )(got_odd, got_even, odd, even, own, wide, wind, couple)
    return out.reshape(lam_end.shape)


def solution(mesh):
    return jax.shard_map(
        body,
        mesh=mesh,
        in_specs=(
            P(None, None, "lat", "lon"),
            P(None, None, "lat", "lon"),
            P(None, None, "lat", "lon"),
            P(("lat", "lon"), None, None, None),
            P(("lat", "lon"), None, None),
            P(("lat", "lon"), None),
        ),
        out_specs=P(None, None, "lat", "lon"),
        check_vma=False,
    )
```

```python
import functools

import jax
import jax.numpy as jnp
from jax import lax
from jax.experimental import pallas as pl
from jax.experimental.pallas import tpu as pltpu
from jax.sharding import PartitionSpec as P

DIFFUSION = 0.1
F32 = jnp.float32
BF16 = jnp.bfloat16

TARGET_ROW = 64
EDGE_ROW = 72
STRIP_ROW = 112
LON_ROWS = 192

A_AT, B_AT, C_AT, STRIP_AT = 16, 18, 19, 23
LAT_ROWS = 24 * 16
SLOTS = {
    **{field: (field * 8, 1, 6) for field in range(4)},
    **{4 + field: (32 + field * 8, 2, 5) for field in range(4)},
    **{8 + field: (112 + (field // 2) * 8 + (field % 2) * 2, 3, 4) for field in range(4)},
    A_AT: (96, 1, 6),
    B_AT: (104, 1, 6),
    **{C_AT + field: (64 + field * 8, 2, 5) for field in range(4)},
}
CENTRE = 1.0 - 4.0 * DIFFUSION


def pieces(values):
    high = values.astype(BF16)
    rest = values - high.astype(F32)
    middle = rest.astype(BF16)
    low = (rest - middle.astype(F32)).astype(BF16)
    return high, middle, low


def lanes_of(rows):
    return lax.broadcasted_iota(jnp.int32, (rows, 128), 1)


def levels(ref, field, row, first=0, count=16):
    return ref[field, pl.ds(first * 8 + row, count, stride=8), :]


def pack_blocks(tile, apart, count_ref, column_ref, values_ref, out_ref):
    slot = lax.broadcasted_iota(jnp.int32, (64, 128), 0)
    cell = lax.broadcasted_iota(jnp.int32, (64, 128), 0)
    side = cell >> 3
    wanted = (cell & 7) * 128 + jnp.where(side < 4, 124 + side, side - 4)
    lane = lanes_of(8)
    allowed = (lanes_of(64) < 64) == (side < 4)
    dest = tile ^ apart
    left, right = (dest + 3) & 3, (dest + 1) & 3
    block = lambda t: jnp.where(slot < count_ref[0, t], values_ref[t], 0.0)
    column = lambda t: column_ref[pl.ds(t, 1), :]
    out_ref[0:64, :] = block(dest)
    wide = jnp.concatenate([column(dest), jnp.zeros((1, 64), jnp.int32)], axis=1)
    out_ref[TARGET_ROW:EDGE_ROW, :] = jnp.broadcast_to(wide.astype(F32), (8, 128))
    target = jnp.concatenate([column(left), column(right)], axis=1)
    hit = jnp.where(jnp.logical_and(jnp.broadcast_to(target, (64, 128)) == wanted, allowed), 1.0, 0.0)
    hit = hit.astype(BF16)
    both = jnp.concatenate([block(left), block(right)], axis=0)
    total = jnp.zeros((64, 128), F32)
    for piece in pieces(both):
        total = total + jnp.dot(hit, piece, preferred_element_type=F32)
    at = [total[c * 8 : c * 8 + 8] for c in range(8)]
    for place, rows in enumerate(
        (
            at[3],
            at[4],
            jnp.where(lane < 32, pltpu.roll(at[0], 32, 1), at[2]),
            jnp.where(lane < 32, pltpu.roll(at[7], 32, 1), at[5]),
            jnp.where(lane < 64, pltpu.roll(at[6], 64, 1), at[1]),
        )
    ):
        out_ref[EDGE_ROW + place * 8 : EDGE_ROW + place * 8 + 8, :] = rows


def own_blocks_kernel(count_ref, column_ref, values_ref, out_ref):
    pack_blocks(lax.axis_index("lon"), 0, count_ref, column_ref, values_ref, out_ref)


def pack_kernel(*refs):
    sources, outs, copies_of, sems = refs[:6], refs[6:9], refs[9:15], refs[15]
    copies = [pltpu.make_async_copy(sources[i], copies_of[i], sems.at[i]) for i in range(6)]
    for i in (2, 1, 0, 3, 5, 4):
        copies[i].start()
    for copy in copies[:3]:
        copy.wait()
    count_ref, column_ref, values_ref, lam_ref, winds_ref, coupling_ref = copies_of
    tile = lax.axis_index("lon")
    lane = lanes_of(8)
    for apart in (3, 2, 1):
        pack_blocks(tile, apart, count_ref, column_ref, values_ref, outs[apart - 1])

    for copy in copies[3:]:
        copy.wait()
    row = STRIP_ROW
    for ref, fields in ((lam_ref, 4), (winds_ref, 2), (coupling_ref, 4)):
        for field in range(fields):
            strip = jnp.zeros((8, 128), F32)
            for half in range(2):
                for r in range(8):
                    at = half * 64 + r * 8
                    moved = pltpu.roll(levels(ref, field, r, half * 8, 8), (at + 4) % 128, 1)
                    strip = jnp.where(jnp.logical_and(lane >= at, lane < at + 8), moved, strip)
            for apart in (1, 3):
                outs[apart - 1][row : row + 8, :] = strip
            row += 8


def slot_mask(plane, way, lane):
    at, first, last = SLOTS[plane]
    place = (lane - (at + way * 72)) & 127
    return jnp.logical_and(place >= first, place <= last)


def once(make):
    made = {}

    def get(*key):
        if key not in made:
            made[key] = make(*key)
        return made[key]

    return get


def along(x, to_left, to_right, beside, at, lane):
    p_right, p_left = to_left * x, to_right * x
    strip_right, strip_left = beside
    right = jnp.where(lane == 127, pltpu.roll(strip_right, (123 - at) % 128, 1), pltpu.roll(p_right, 127, 1))
    left = jnp.where(lane == 0, pltpu.roll(strip_left, (125 - at) % 128, 1), pltpu.roll(p_left, 1, 1))
    return right + left, (p_right, p_left)


def insert(inner, pair, at, lane):
    p_right, p_left = pair
    inner = jnp.where(lane == at + 3, pltpu.roll(p_right, (at + 3) % 128, 1), inner)
    return jnp.where(lane == at + 4, pltpu.roll(p_left, (at + 5) % 128, 1), inner)


def strip_along(rolled_right, rolled_left, inner, side):
    right = jnp.where(side == 3, inner, rolled_right)
    left = jnp.where(side == 4, inner, rolled_left)
    return right + left


def own_steps(lam_ref, winds_ref, coupling_ref, force_ref, strips_ref, wanted, keep):
    lane = lanes_of(8)
    side = lane & 7
    strip_row = (lane >> 3) & 7

    def force(row, instant, field, half):
        at = instant * 32 + field * 16 + half * 8
        return force_ref[row, at : at + 8, :]

    half_wind = once(lambda axis, row, half: 0.5 * levels(winds_ref, axis, row, half * 8, 8))
    up_weight = once(lambda row, half: DIFFUSION + half_wind(0, row, half))
    down_weight = once(lambda row, half: DIFFUSION - half_wind(0, row, half))
    right_weight = once(lambda row, half: DIFFUSION + half_wind(1, row, half))
    left_weight = once(lambda row, half: DIFFUSION - half_wind(1, row, half))

    def strip(place):
        return strips_ref[place * 8 : place * 8 + 8, :]

    half_a, half_b = 0.5 * strip(4), 0.5 * strip(5)
    strip_up, strip_down = DIFFUSION + half_a, DIFFUSION - half_a
    strip_right, strip_left = DIFFUSION + half_b, DIFFUSION - half_b

    u = [{}, {}, {}, {}]
    for field in range(4):
        for half in range(2):
            for row in range(8):
                value = levels(lam_ref, field, row, half * 8, 8)
                if field >= 2:
                    value = value + force(row, 3, field - 2, half)
                u[field][row, half] = value
    strips = [strip(field) for field in range(4)]
    keep(0, u, strips)
    for step, rows in enumerate(wanted, 1):
        last = step == 4
        later = [{}, {}, {}, {}]
        later_strips = []
        for field in range(4):
            x = u[field]
            beside = (strip_right * strips[field], strip_left * strips[field])
            rolled_right = pltpu.roll(beside[0], 127, 1)
            rolled_left = pltpu.roll(beside[1], 1, 1)
            inner = beside[0]
            for half in range(2):
                for row in rows:
                    at = half * 64 + row * 8
                    shares, pair = along(
                        x[row, half], right_weight(row, half), left_weight(row, half), beside, at, lane
                    )
                    total = CENTRE * x[row, half] + shares
                    if row < 7:
                        total = total + up_weight(row + 1, half) * x[row + 1, half]
                    if row > 0:
                        total = total + down_weight(row - 1, half) * x[row - 1, half]
                    if field < 2:
                        first = levels(coupling_ref, field, row, half * 8, 8)
                        second = levels(coupling_ref, field + 2, row, half * 8, 8)
                        total = total - (first * u[2][row, half] + second * u[3][row, half])
                    elif not last:
                        total = total + force(row, 3 - step, field - 2, half)
                    later[field][row, half] = total
                    if not last:
                        inner = insert(inner, pair, at, lane)
            if not last:
                total = CENTRE * strips[field] + strip_along(rolled_right, rolled_left, inner, side)
                total = total + jnp.where(strip_row == 7, 0.0, pltpu.roll(strip_up * strips[field], 120, 1))
                total = total + jnp.where(strip_row == 0, 0.0, pltpu.roll(strip_down * strips[field], 8, 1))
                if field < 2:
                    total = total - (strip(6 + field) * strips[2] + strip(8 + field) * strips[3])
                else:
                    total = total + strip(10 + 2 * (step - 1) + field - 2)
                later_strips.append(total)
        u, strips = later, later_strips
        keep(step, u, strips)


def halo_kernel(
    got3_ref, got2_ref, got1_ref, own_ref, lam_ref, winds_ref, coupling_ref, even_ref, odd_ref, force_ref, strips_ref, edge_ref
):
    is_even = lax.rem(lax.axis_index("lat"), 2) == 0
    right_is_1 = lax.rem(lax.axis_index("lon"), 2) == 0
    lane = lanes_of(8)
    lane1 = lanes_of(1)
    messages = (own_ref, got1_ref, got2_ref, got3_ref)

    rows = [message[TARGET_ROW : TARGET_ROW + 1, :] for message in messages]
    halves = [jnp.where(lane1 < 64, rows[s], pltpu.roll(rows[s + 1], 64, 1)) for s in (0, 2)]
    target = jnp.concatenate(halves, axis=1).astype(jnp.int32)
    blocks = jnp.concatenate([message[0:64, :] for message in messages], axis=0)
    stacked = jnp.concatenate(pieces(blocks.T), axis=0)
    cell = lax.broadcasted_iota(jnp.int32, (256, 256), 0)
    for pair in range(4):
        hit = jnp.where(jnp.broadcast_to(target, (256, 256)) == cell + pair * 256, 1.0, 0.0).astype(BF16)
        three = lax.dot_general(stacked, hit, (((1,), (1,)), ((), ())), preferred_element_type=F32)
        both = three[0:128] + three[128:256] + three[256:384]
        force_ref[2 * pair] = both[:, 0:128]
        force_ref[2 * pair + 1] = both[:, 128:256]

    near2, near1, far24, far42, thirds = [
        sum(message[EDGE_ROW + place * 8 : EDGE_ROW + place * 8 + 8, :] for message in messages)
        for place in (0, 1, 2, 3, 4)
    ]
    for c, rows in enumerate(
        (
            jnp.where(lane >= 96, pltpu.roll(far24, 96, 1), 0.0),
            jnp.where(lane >= 64, thirds, 0.0),
            jnp.where(lane >= 32, far24, 0.0),
            near2,
            near1,
            jnp.where(lane >= 32, far42, 0.0),
            jnp.where(lane >= 64, pltpu.roll(thirds, 64, 1), 0.0),
            jnp.where(lane >= 96, pltpu.roll(far42, 96, 1), 0.0),
        )
    ):
        edge_ref[pl.ds(c, 8, stride=8), :] = rows
        edge_ref[pl.ds(64 + c, 8, stride=8), :] = rows
    edge = edge_ref[...].T

    def edge_strip(instant, field):
        at = instant * 32 + field * 16
        return jnp.where(lane < 64, edge[at : at + 8], edge[at + 8 : at + 16])

    from_1 = ((lane & 7) < 4) != right_is_1
    for field in range(10):
        at = STRIP_ROW + field * 8
        strip = jnp.where(from_1, got1_ref[at : at + 8, :], got3_ref[at : at + 8, :])
        if field in (2, 3):
            strip = strip + edge_strip(3, field - 2)
        strips_ref[field * 8 : field * 8 + 8, :] = strip
    for place, (instant, field) in enumerate(((2, 0), (2, 1), (1, 0), (1, 1), (0, 0), (0, 1))):
        strips_ref[80 + place * 8 : 88 + place * 8, :] = edge_strip(instant, field)

    sides = {}

    def put(plane, half, up, down):
        at = plane * 16 + half * 8
        even_ref[at : at + 8, :] = jnp.where(is_even, up, down)
        odd_ref[at : at + 8, :] = jnp.where(is_even, down, up)

    def put_strip(plane, packed):
        for half in range(2):
            for way, row in ((0, 7), (1, 0)):
                at = SLOTS[plane][0] + way * 72
                moved = pltpu.roll(packed, (at - half * 64 - row * 8) % 128, 1)
                sides[half, way] = jnp.where(slot_mask(plane, way, lane), moved, sides.get((half, way), 0.0))

    def keep(step, u, strips):
        for field in range(4):
            plane = step * 4 + field
            for half in range(2):
                put(plane, half, u[field][7, half], u[field][0, half])
            if step < 3:
                put_strip(plane, strips[field])

    own_steps(
        lam_ref,
        winds_ref,
        coupling_ref,
        force_ref,
        strips_ref,
        ((0, 1, 2, 5, 6, 7), (0, 1, 6, 7), (0, 7)),
        keep,
    )
    for plane, ref, field, depth in (
        (A_AT, winds_ref, 0, 0),
        (A_AT + 1, winds_ref, 0, 1),
        (B_AT, winds_ref, 1, 0),
        (C_AT, coupling_ref, 0, 0),
        (C_AT + 1, coupling_ref, 1, 0),
        (C_AT + 2, coupling_ref, 2, 0),
        (C_AT + 3, coupling_ref, 3, 0),
    ):
        for half in range(2):
            put(plane, half, levels(ref, field, 7 - depth, half * 8, 8), levels(ref, field, depth, half * 8, 8))
        if depth == 0:
            place = field + (4 if ref is winds_ref else 6)
            put_strip(plane, strips_ref[place * 8 : place * 8 + 8, :])
    for half in range(2):
        put(STRIP_AT, half, sides[half, 0], sides[half, 1])


def own_kernel(force_ref, strips_ref, lam_ref, winds_ref, coupling_ref, out_ref, wide_ref):
    every = tuple(range(8))

    def widen(place, packed):
        for half in range(2):
            at = (place * 2 + half) * 8
            wide_ref[at : at + 8, :] = pltpu.roll(packed, 16 if half == 0 else 80, 1)

    def keep(step, u, strips):
        for field in range(4):
            if step < 3:
                widen(step * 4 + field, strips[field])
            if step == 4:
                for half in range(2):
                    for row in range(8):
                        out_ref[field, row, half * 8 : half * 8 + 8, :] = u[field][row, half]

    for place in range(6):
        widen(12 + place, strips_ref[32 + place * 8 : 40 + place * 8, :])
    own_steps(lam_ref, winds_ref, coupling_ref, force_ref, strips_ref, (every,) * 4, keep)


def join_kernel(
    bands,
    odd_ref,
    even_ref,
    sent_odd_ref,
    sent_even_ref,
    own_ref,
    wide_ref,
    winds_ref,
    coupling_ref,
    out_ref,
    border_ref,
):
    band = lax.axis_index("lat")
    is_even = lax.rem(band, 2) == 0
    low_mask = jnp.where(band > 0, 1.0, 0.0).astype(F32)
    high_mask = jnp.where(band < bands - 1, 1.0, 0.0).astype(F32)
    lane = lanes_of(8)
    side = lane & 7
    strip_row = (lane >> 3) - 2
    strip_mask = jnp.where(strip_row < 0, low_mask, jnp.where(strip_row > 7, high_mask, 1.0))

    def chosen(first, second):
        def get(plane, half):
            at = plane * 16 + half * 8
            return jnp.where(is_even, first[at : at + 8, :], second[at : at + 8, :])

        return once(get)

    low, high = chosen(odd_ref, even_ref), chosen(even_ref, odd_ref)
    up, down = chosen(sent_even_ref, sent_odd_ref), chosen(sent_odd_ref, sent_even_ref)
    border_of = {-1: low, 0: down, 7: up, 8: high}

    def outer(first, row, half, own):
        if row < 0:
            return low(first - 1 - row, half)
        if row > 7:
            return high(first + row - 8, half)
        return own

    def half_wind(axis, row, half):
        own = levels(winds_ref, axis, row, half * 8, 8) if 0 <= row <= 7 else None
        return 0.5 * outer(A_AT if axis == 0 else B_AT, row, half, own)

    half_wind = once(half_wind)
    up_weight = once(lambda row, half: DIFFUSION + half_wind(0, row, half))
    down_weight = once(lambda row, half: DIFFUSION - half_wind(0, row, half))
    right_weight = once(lambda row, half: DIFFUSION + half_wind(1, row, half))
    left_weight = once(lambda row, half: DIFFUSION - half_wind(1, row, half))

    def couple(field, row, half):
        own = levels(coupling_ref, field, row, half * 8, 8) if 0 <= row <= 7 else None
        return outer(C_AT + field, row, half, own)

    couple = once(couple)

    def met(plane, half):
        both = jnp.where(slot_mask(plane, 0, lane), low(STRIP_AT, half), high(STRIP_AT, half))
        return pltpu.roll(both, (8 - SLOTS[plane][0]) % 128, 1)

    inside = jnp.logical_and(strip_row >= 0, strip_row <= 7)

    def strip(place, plane, half):
        at = (place * 2 + half) * 8
        return jnp.where(inside, wide_ref[at : at + 8, :], met(plane, half))

    for plane in range(12):
        for half in range(2):
            at = (plane * 2 + half) * 8
            border_ref[at : at + 8, :] = strip(plane, plane, half)
    strip_a = [0.5 * strip(12, A_AT, half) for half in range(2)]
    strip_b = [0.5 * strip(13, B_AT, half) for half in range(2)]
    strip_c = [[strip(14 + field, C_AT + field, half) for half in range(2)] for field in range(4)]

    e = [{}, {}, {}, {}]
    strips = [[None, None] for _ in range(4)]
    reach = ((-1, 0), (-2, -1, 0, 1), (-1, 0, 1, 2), (0, 1, 2, 3))
    for step in range(4):
        last = step == 3
        rows = reach[step] + tuple(7 - row for row in reach[step])
        later = [{}, {}, {}, {}]
        later_strips = [[None, None] for _ in range(4)]
        for field in range(4):
            x = e[field]
            plane = step * 4 + field
            for half in range(2):
                xs = strips[field][half]
                if step > 0:
                    beside = ((DIFFUSION + strip_b[half]) * xs, (DIFFUSION - strip_b[half]) * xs)
                    rolled_right = pltpu.roll(beside[0], 127, 1)
                    rolled_left = pltpu.roll(beside[1], 1, 1)
                    inner = beside[0]
                for row in rows:
                    terms = []
                    if (row, half) in x:
                        here = x[row, half]
                        at = (row + 2) * 8
                        shares, pair = along(
                            here, right_weight(row, half), left_weight(row, half), beside, at, lane
                        )
                        local = CENTRE * here + shares
                        if field < 2:
                            local = local - (
                                couple(field, row, half) * e[2][row, half]
                                + couple(field + 2, row, half) * e[3][row, half]
                            )
                        terms.append(local)
                        if not last:
                            inner = insert(inner, pair, at, lane)
                    for near, crossing, weight in (
                        (row + 1, (0, 8), up_weight),
                        (row - 1, (-1, 7), down_weight),
                    ):
                        parts = []
                        if (near, half) in x:
                            parts.append(x[near, half])
                        if near in crossing:
                            parts.append(border_of[near](plane, half))
                        if parts:
                            terms.append(weight(near, half) * sum(parts[1:], parts[0]))
                    total = sum(terms[1:], terms[0])
                    if row == -1:
                        total = total * low_mask
                    if row == 8:
                        total = total * high_mask
                    if last:
                        total = total + own_ref[field, row, half * 8 : half * 8 + 8, :]
                        out_ref[field, pl.ds(half * 64 + row, 8, stride=8), :] = total
                    else:
                        later[field][row, half] = total
                if not last:
                    at = (plane * 2 + half) * 8
                    border = border_ref[at : at + 8, :]
                    from_above = jnp.where(jnp.logical_or(strip_row == 0, strip_row == 8), border, 0.0)
                    from_below = jnp.where(jnp.logical_or(strip_row == -1, strip_row == 7), border, 0.0)
                    if step > 0:
                        from_above, from_below = from_above + xs, from_below + xs
                    total = pltpu.roll((DIFFUSION + strip_a[half]) * from_above, 120, 1)
                    total = total + pltpu.roll((DIFFUSION - strip_a[half]) * from_below, 8, 1)
                    if step > 0:
                        total = total + CENTRE * xs + strip_along(rolled_right, rolled_left, inner, side)
                        if field < 2:
                            total = total - (
                                strip_c[field][half] * strips[2][half] + strip_c[field + 2][half] * strips[3][half]
                            )
                    later_strips[field][half] = total * strip_mask
        e, strips = later, later_strips


def vmem(count):
    return [pl.BlockSpec(memory_space=pltpu.VMEM)] * count


def params(mebibytes=24):
    return pltpu.CompilerParams(vmem_limit_bytes=mebibytes * 1024 * 1024)


def body(lam_end, winds, coupling, obs_values, obs_column, obs_count):
    bands = lax.axis_size("lat")
    tiles = lax.axis_size("lon")
    lam = lam_end.reshape(4, 128, 128)
    wind = winds.reshape(2, 128, 128)
    couple = coupling.reshape(4, 128, 128)

    lon_rows = (LON_ROWS, STRIP_ROW, LON_ROWS)
    parts = pl.pallas_call(
        pack_kernel,
        out_shape=tuple(jax.ShapeDtypeStruct((rows, 128), F32) for rows in lon_rows),
        in_specs=[pl.BlockSpec(memory_space=pltpu.HBM)] * 6,
        out_specs=tuple(vmem(3)),
        scratch_shapes=[
            pltpu.SMEM((1, 4), jnp.int32),
            pltpu.VMEM((4, 64), jnp.int32),
            pltpu.VMEM((4, 64, 128), F32),
            pltpu.VMEM((4, 128, 128), F32),
            pltpu.VMEM((2, 128, 128), F32),
            pltpu.VMEM((4, 128, 128), F32),
            pltpu.SemaphoreType.DMA((6,)),
        ],
        compiler_params=pltpu.CompilerParams(vmem_limit_bytes=54950 * 1024),
        name="pack_blocks_and_strips",
    )(obs_count, obs_column[0], obs_values[0], lam, wind, couple)
    got3, got2, got1 = [
        lax.ppermute(parts[apart - 1], "lon", [(i, i ^ apart) for i in range(tiles)]) for apart in (3, 2, 1)
    ]

    own_part = pl.pallas_call(
        own_blocks_kernel,
        out_shape=jax.ShapeDtypeStruct((STRIP_ROW, 128), F32),
        in_specs=[pl.BlockSpec(memory_space=pltpu.SMEM)] + vmem(2),
        out_specs=vmem(1)[0],
        compiler_params=params(),
        cost_estimate=pl.CostEstimate(flops=5_000_000, bytes_accessed=1_000_000, transcendentals=0),
        name="own_blocks",
    )(obs_count, obs_column[0], obs_values[0])

    halo = jax.ShapeDtypeStruct((LAT_ROWS, 128), F32)
    even, odd, force, strips = pl.pallas_call(
        halo_kernel,
        out_shape=(
            halo,
            halo,
            jax.ShapeDtypeStruct((8, 128, 128), F32),
            jax.ShapeDtypeStruct((128, 128), F32),
        ),
        in_specs=vmem(7),
        out_specs=tuple(vmem(4)),
        scratch_shapes=[pltpu.VMEM((128, 128), F32)],
        compiler_params=params(),
        name="scatter_and_halo",
    )(got3, got2, got1, own_part, lam, wind, couple)
    swap = lambda first: [p for i in range(first, bands - 1, 2) for p in ((i, i + 1), (i + 1, i))]
    got_odd = lax.ppermute(odd, "lat", swap(1))
    got_even = lax.ppermute(even, "lat", swap(0))

    own, wide = pl.pallas_call(
        own_kernel,
        out_shape=(jax.ShapeDtypeStruct((4, 8, 16, 128), F32), jax.ShapeDtypeStruct((288, 128), F32)),
        in_specs=vmem(5),
        out_specs=tuple(vmem(2)),
        compiler_params=params(),
        cost_estimate=pl.CostEstimate(flops=10_000_000, bytes_accessed=2_000_000, transcendentals=0),
        name="own_steps",
    )(force, strips, lam, wind, couple)

    out = pl.pallas_call(
        functools.partial(join_kernel, bands),
        out_shape=jax.ShapeDtypeStruct((4, 128, 128), F32),
        in_specs=vmem(8),
        out_specs=vmem(1)[0],
        scratch_shapes=[pltpu.VMEM((192, 128), F32)],
        compiler_params=params(),
        name="join_bands",
    )(got_odd, got_even, odd, even, own, wide, wind, couple)
    return out.reshape(lam_end.shape)


def solution(mesh):
    return jax.shard_map(
        body,
        mesh=mesh,
        in_specs=(
            P(None, None, "lat", "lon"),
            P(None, None, "lat", "lon"),
            P(None, None, "lat", "lon"),
            P(("lat", "lon"), None, None, None),
            P(("lat", "lon"), None, None),
            P(("lat", "lon"), None),
        ),
        out_specs=P(None, None, "lat", "lon"),
        check_vma=False,
    )
```

```python
import functools

import jax
import jax.numpy as jnp
from jax import lax
from jax.experimental import pallas as pl
from jax.experimental.pallas import tpu as pltpu
from jax.sharding import PartitionSpec as P

DIFFUSION = 0.1
F32 = jnp.float32
BF16 = jnp.bfloat16

TARGET_ROW = 64
EDGE_ROW = 72
STRIP_ROW = 112
LON_ROWS = 192

A_AT, B_AT, C_AT, STRIP_AT = 16, 18, 19, 23
LAT_ROWS = 24 * 16
SLOTS = {
    **{field: (field * 8, 1, 6) for field in range(4)},
    **{4 + field: (32 + field * 8, 2, 5) for field in range(4)},
    **{8 + field: (112 + (field // 2) * 8 + (field % 2) * 2, 3, 4) for field in range(4)},
    A_AT: (96, 1, 6),
    B_AT: (104, 1, 6),
    **{C_AT + field: (64 + field * 8, 2, 5) for field in range(4)},
}
CENTRE = 1.0 - 4.0 * DIFFUSION


def pieces(values):
    high = values.astype(BF16)
    rest = values - high.astype(F32)
    middle = rest.astype(BF16)
    low = (rest - middle.astype(F32)).astype(BF16)
    return high, middle, low


def lanes_of(rows):
    return lax.broadcasted_iota(jnp.int32, (rows, 128), 1)


def levels(ref, field, row, first=0, count=16):
    return ref[field, pl.ds(first * 8 + row, count, stride=8), :]


def pack_blocks(tile, apart, count_ref, column_ref, values_ref, out_ref):
    slot = lax.broadcasted_iota(jnp.int32, (64, 128), 0)
    cell = lax.broadcasted_iota(jnp.int32, (64, 128), 0)
    side = cell >> 3
    wanted = (cell & 7) * 128 + jnp.where(side < 4, 124 + side, side - 4)
    lane = lanes_of(8)
    allowed = (lanes_of(64) < 64) == (side < 4)
    dest = tile ^ apart
    left, right = (dest + 3) & 3, (dest + 1) & 3
    block = lambda t: jnp.where(slot < count_ref[0, t], values_ref[t], 0.0)
    column = lambda t: column_ref[pl.ds(t, 1), :]
    out_ref[0:64, :] = block(dest)
    wide = jnp.concatenate([column(dest), jnp.zeros((1, 64), jnp.int32)], axis=1)
    out_ref[TARGET_ROW:EDGE_ROW, :] = jnp.broadcast_to(wide.astype(F32), (8, 128))
    target = jnp.concatenate([column(left), column(right)], axis=1)
    hit = jnp.where(jnp.logical_and(jnp.broadcast_to(target, (64, 128)) == wanted, allowed), 1.0, 0.0)
    hit = hit.astype(BF16)
    both = jnp.concatenate([block(left), block(right)], axis=0)
    total = jnp.zeros((64, 128), F32)
    for piece in pieces(both):
        total = total + jnp.dot(hit, piece, preferred_element_type=F32)
    at = [total[c * 8 : c * 8 + 8] for c in range(8)]
    for place, rows in enumerate(
        (
            at[3],
            at[4],
            jnp.where(lane < 32, pltpu.roll(at[0], 32, 1), at[2]),
            jnp.where(lane < 32, pltpu.roll(at[7], 32, 1), at[5]),
            jnp.where(lane < 64, pltpu.roll(at[6], 64, 1), at[1]),
        )
    ):
        out_ref[EDGE_ROW + place * 8 : EDGE_ROW + place * 8 + 8, :] = rows


def own_blocks_kernel(count_ref, column_ref, values_ref, out_ref):
    pack_blocks(lax.axis_index("lon"), 0, count_ref, column_ref, values_ref, out_ref)


def pack_kernel(*refs):
    sources, outs, copies_of, sems = refs[:6], refs[6:9], refs[9:15], refs[15]
    copies = [pltpu.make_async_copy(sources[i], copies_of[i], sems.at[i]) for i in range(6)]
    for i in (2, 1, 0, 3, 5, 4):
        copies[i].start()
    for copy in copies[:3]:
        copy.wait()
    count_ref, column_ref, values_ref, lam_ref, winds_ref, coupling_ref = copies_of
    tile = lax.axis_index("lon")
    lane = lanes_of(8)
    for apart in (3, 2, 1):
        pack_blocks(tile, apart, count_ref, column_ref, values_ref, outs[apart - 1])

    for copy in copies[3:]:
        copy.wait()
    row = STRIP_ROW
    for ref, fields in ((lam_ref, 4), (winds_ref, 2), (coupling_ref, 4)):
        for field in range(fields):
            strip = jnp.zeros((8, 128), F32)
            for half in range(2):
                for r in range(8):
                    at = half * 64 + r * 8
                    moved = pltpu.roll(levels(ref, field, r, half * 8, 8), (at + 4) % 128, 1)
                    strip = jnp.where(jnp.logical_and(lane >= at, lane < at + 8), moved, strip)
            for apart in (1, 3):
                outs[apart - 1][row : row + 8, :] = strip
            row += 8


def slot_mask(plane, way, lane):
    at, first, last = SLOTS[plane]
    place = (lane - (at + way * 72)) & 127
    return jnp.logical_and(place >= first, place <= last)


def once(make):
    made = {}

    def get(*key):
        if key not in made:
            made[key] = make(*key)
        return made[key]

    return get


def along(x, to_left, to_right, beside, at, lane):
    p_right, p_left = to_left * x, to_right * x
    strip_right, strip_left = beside
    right = jnp.where(lane == 127, pltpu.roll(strip_right, (123 - at) % 128, 1), pltpu.roll(p_right, 127, 1))
    left = jnp.where(lane == 0, pltpu.roll(strip_left, (125 - at) % 128, 1), pltpu.roll(p_left, 1, 1))
    return right + left, (p_right, p_left)


def insert(inner, pair, at, lane):
    p_right, p_left = pair
    inner = jnp.where(lane == at + 3, pltpu.roll(p_right, (at + 3) % 128, 1), inner)
    return jnp.where(lane == at + 4, pltpu.roll(p_left, (at + 5) % 128, 1), inner)


def strip_along(rolled_right, rolled_left, inner, side):
    right = jnp.where(side == 3, inner, rolled_right)
    left = jnp.where(side == 4, inner, rolled_left)
    return right + left


def own_steps(lam_ref, winds_ref, coupling_ref, force_ref, strips_ref, wanted, keep):
    lane = lanes_of(8)
    side = lane & 7
    strip_row = (lane >> 3) & 7

    def force(row, instant, field, half):
        at = instant * 32 + field * 16 + half * 8
        return force_ref[row, at : at + 8, :]

    half_wind = once(lambda axis, row, half: 0.5 * levels(winds_ref, axis, row, half * 8, 8))
    up_weight = once(lambda row, half: DIFFUSION + half_wind(0, row, half))
    down_weight = once(lambda row, half: DIFFUSION - half_wind(0, row, half))
    right_weight = once(lambda row, half: DIFFUSION + half_wind(1, row, half))
    left_weight = once(lambda row, half: DIFFUSION - half_wind(1, row, half))

    def strip(place):
        return strips_ref[place * 8 : place * 8 + 8, :]

    half_a, half_b = 0.5 * strip(4), 0.5 * strip(5)
    strip_up, strip_down = DIFFUSION + half_a, DIFFUSION - half_a
    strip_right, strip_left = DIFFUSION + half_b, DIFFUSION - half_b

    u = [{}, {}, {}, {}]
    for field in range(4):
        for half in range(2):
            for row in range(8):
                value = levels(lam_ref, field, row, half * 8, 8)
                if field >= 2:
                    value = value + force(row, 3, field - 2, half)
                u[field][row, half] = value
    strips = [strip(field) for field in range(4)]
    keep(0, u, strips)
    for step, rows in enumerate(wanted, 1):
        last = step == 4
        later = [{}, {}, {}, {}]
        later_strips = []
        for field in range(4):
            x = u[field]
            beside = (strip_right * strips[field], strip_left * strips[field])
            rolled_right = pltpu.roll(beside[0], 127, 1)
            rolled_left = pltpu.roll(beside[1], 1, 1)
            inner = beside[0]
            for half in range(2):
                for row in rows:
                    at = half * 64 + row * 8
                    shares, pair = along(
                        x[row, half], right_weight(row, half), left_weight(row, half), beside, at, lane
                    )
                    total = CENTRE * x[row, half] + shares
                    if row < 7:
                        total = total + up_weight(row + 1, half) * x[row + 1, half]
                    if row > 0:
                        total = total + down_weight(row - 1, half) * x[row - 1, half]
                    if field < 2:
                        first = levels(coupling_ref, field, row, half * 8, 8)
                        second = levels(coupling_ref, field + 2, row, half * 8, 8)
                        total = total - (first * u[2][row, half] + second * u[3][row, half])
                    elif not last:
                        total = total + force(row, 3 - step, field - 2, half)
                    later[field][row, half] = total
                    if not last:
                        inner = insert(inner, pair, at, lane)
            if not last:
                total = CENTRE * strips[field] + strip_along(rolled_right, rolled_left, inner, side)
                total = total + jnp.where(strip_row == 7, 0.0, pltpu.roll(strip_up * strips[field], 120, 1))
                total = total + jnp.where(strip_row == 0, 0.0, pltpu.roll(strip_down * strips[field], 8, 1))
                if field < 2:
                    total = total - (strip(6 + field) * strips[2] + strip(8 + field) * strips[3])
                else:
                    total = total + strip(10 + 2 * (step - 1) + field - 2)
                later_strips.append(total)
        u, strips = later, later_strips
        keep(step, u, strips)


def halo_kernel(
    got2_ref, got3_ref, got1_ref, own_ref, lam_ref, winds_ref, coupling_ref, even_ref, odd_ref, force_ref, strips_ref, edge_ref
):
    is_even = lax.rem(lax.axis_index("lat"), 2) == 0
    right_is_1 = lax.rem(lax.axis_index("lon"), 2) == 0
    lane = lanes_of(8)
    lane1 = lanes_of(1)
    messages = (own_ref, got1_ref, got2_ref, got3_ref)

    rows = [message[TARGET_ROW : TARGET_ROW + 1, :] for message in messages]
    halves = [jnp.where(lane1 < 64, rows[s], pltpu.roll(rows[s + 1], 64, 1)) for s in (0, 2)]
    target = jnp.concatenate(halves, axis=1).astype(jnp.int32)
    blocks = jnp.concatenate([message[0:64, :] for message in messages], axis=0)
    stacked = jnp.concatenate(pieces(blocks.T), axis=0)
    cell = lax.broadcasted_iota(jnp.int32, (256, 256), 0)
    for pair in range(4):
        hit = jnp.where(jnp.broadcast_to(target, (256, 256)) == cell + pair * 256, 1.0, 0.0).astype(BF16)
        three = lax.dot_general(stacked, hit, (((1,), (1,)), ((), ())), preferred_element_type=F32)
        both = three[0:128] + three[128:256] + three[256:384]
        force_ref[2 * pair] = both[:, 0:128]
        force_ref[2 * pair + 1] = both[:, 128:256]

    near2, near1, far24, far42, thirds = [
        sum(message[EDGE_ROW + place * 8 : EDGE_ROW + place * 8 + 8, :] for message in messages)
        for place in (0, 1, 2, 3, 4)
    ]
    for c, rows in enumerate(
        (
            jnp.where(lane >= 96, pltpu.roll(far24, 96, 1), 0.0),
            jnp.where(lane >= 64, thirds, 0.0),
            jnp.where(lane >= 32, far24, 0.0),
            near2,
            near1,
            jnp.where(lane >= 32, far42, 0.0),
            jnp.where(lane >= 64, pltpu.roll(thirds, 64, 1), 0.0),
            jnp.where(lane >= 96, pltpu.roll(far42, 96, 1), 0.0),
        )
    ):
        edge_ref[pl.ds(c, 8, stride=8), :] = rows
        edge_ref[pl.ds(64 + c, 8, stride=8), :] = rows
    edge = edge_ref[...].T

    def edge_strip(instant, field):
        at = instant * 32 + field * 16
        return jnp.where(lane < 64, edge[at : at + 8], edge[at + 8 : at + 16])

    from_1 = ((lane & 7) < 4) != right_is_1
    for field in range(10):
        at = STRIP_ROW + field * 8
        strip = jnp.where(from_1, got1_ref[at : at + 8, :], got3_ref[at : at + 8, :])
        if field in (2, 3):
            strip = strip + edge_strip(3, field - 2)
        strips_ref[field * 8 : field * 8 + 8, :] = strip
    for place, (instant, field) in enumerate(((2, 0), (2, 1), (1, 0), (1, 1), (0, 0), (0, 1))):
        strips_ref[80 + place * 8 : 88 + place * 8, :] = edge_strip(instant, field)

    sides = {}

    def put(plane, half, up, down):
        at = plane * 16 + half * 8
        even_ref[at : at + 8, :] = jnp.where(is_even, up, down)
        odd_ref[at : at + 8, :] = jnp.where(is_even, down, up)

    def put_strip(plane, packed):
        for half in range(2):
            for way, row in ((0, 7), (1, 0)):
                at = SLOTS[plane][0] + way * 72
                moved = pltpu.roll(packed, (at - half * 64 - row * 8) % 128, 1)
                sides[half, way] = jnp.where(slot_mask(plane, way, lane), moved, sides.get((half, way), 0.0))

    def keep(step, u, strips):
        for field in range(4):
            plane = step * 4 + field
            for half in range(2):
                put(plane, half, u[field][7, half], u[field][0, half])
            if step < 3:
                put_strip(plane, strips[field])

    own_steps(
        lam_ref,
        winds_ref,
        coupling_ref,
        force_ref,
        strips_ref,
        ((0, 1, 2, 5, 6, 7), (0, 1, 6, 7), (0, 7)),
        keep,
    )
    for plane, ref, field, depth in (
        (A_AT, winds_ref, 0, 0),
        (A_AT + 1, winds_ref, 0, 1),
        (B_AT, winds_ref, 1, 0),
        (C_AT, coupling_ref, 0, 0),
        (C_AT + 1, coupling_ref, 1, 0),
        (C_AT + 2, coupling_ref, 2, 0),
        (C_AT + 3, coupling_ref, 3, 0),
    ):
        for half in range(2):
            put(plane, half, levels(ref, field, 7 - depth, half * 8, 8), levels(ref, field, depth, half * 8, 8))
        if depth == 0:
            place = field + (4 if ref is winds_ref else 6)
            put_strip(plane, strips_ref[place * 8 : place * 8 + 8, :])
    for half in range(2):
        put(STRIP_AT, half, sides[half, 0], sides[half, 1])


def own_kernel(force_ref, strips_ref, lam_ref, winds_ref, coupling_ref, out_ref, wide_ref):
    every = tuple(range(8))

    def widen(place, packed):
        for half in range(2):
            at = (place * 2 + half) * 8
            wide_ref[at : at + 8, :] = pltpu.roll(packed, 16 if half == 0 else 80, 1)

    def keep(step, u, strips):
        for field in range(4):
            if step < 3:
                widen(step * 4 + field, strips[field])
            if step == 4:
                for half in range(2):
                    for row in range(8):
                        out_ref[field, row, half * 8 : half * 8 + 8, :] = u[field][row, half]

    for place in range(6):
        widen(12 + place, strips_ref[32 + place * 8 : 40 + place * 8, :])
    own_steps(lam_ref, winds_ref, coupling_ref, force_ref, strips_ref, (every,) * 4, keep)


def join_kernel(
    bands,
    odd_ref,
    even_ref,
    sent_odd_ref,
    sent_even_ref,
    own_ref,
    wide_ref,
    winds_ref,
    coupling_ref,
    out_ref,
    border_ref,
):
    band = lax.axis_index("lat")
    is_even = lax.rem(band, 2) == 0
    low_mask = jnp.where(band > 0, 1.0, 0.0).astype(F32)
    high_mask = jnp.where(band < bands - 1, 1.0, 0.0).astype(F32)
    lane = lanes_of(8)
    side = lane & 7
    strip_row = (lane >> 3) - 2
    strip_mask = jnp.where(strip_row < 0, low_mask, jnp.where(strip_row > 7, high_mask, 1.0))

    def chosen(first, second):
        def get(plane, half):
            at = plane * 16 + half * 8
            return jnp.where(is_even, first[at : at + 8, :], second[at : at + 8, :])

        return once(get)

    low, high = chosen(odd_ref, even_ref), chosen(even_ref, odd_ref)
    up, down = chosen(sent_even_ref, sent_odd_ref), chosen(sent_odd_ref, sent_even_ref)
    border_of = {-1: low, 0: down, 7: up, 8: high}

    def outer(first, row, half, own):
        if row < 0:
            return low(first - 1 - row, half)
        if row > 7:
            return high(first + row - 8, half)
        return own

    def half_wind(axis, row, half):
        own = levels(winds_ref, axis, row, half * 8, 8) if 0 <= row <= 7 else None
        return 0.5 * outer(A_AT if axis == 0 else B_AT, row, half, own)

    half_wind = once(half_wind)
    up_weight = once(lambda row, half: DIFFUSION + half_wind(0, row, half))
    down_weight = once(lambda row, half: DIFFUSION - half_wind(0, row, half))
    right_weight = once(lambda row, half: DIFFUSION + half_wind(1, row, half))
    left_weight = once(lambda row, half: DIFFUSION - half_wind(1, row, half))

    def couple(field, row, half):
        own = levels(coupling_ref, field, row, half * 8, 8) if 0 <= row <= 7 else None
        return outer(C_AT + field, row, half, own)

    couple = once(couple)

    def met(plane, half):
        both = jnp.where(slot_mask(plane, 0, lane), low(STRIP_AT, half), high(STRIP_AT, half))
        return pltpu.roll(both, (8 - SLOTS[plane][0]) % 128, 1)

    inside = jnp.logical_and(strip_row >= 0, strip_row <= 7)

    def strip(place, plane, half):
        at = (place * 2 + half) * 8
        return jnp.where(inside, wide_ref[at : at + 8, :], met(plane, half))

    for plane in range(12):
        for half in range(2):
            at = (plane * 2 + half) * 8
            border_ref[at : at + 8, :] = strip(plane, plane, half)
    strip_a = [0.5 * strip(12, A_AT, half) for half in range(2)]
    strip_b = [0.5 * strip(13, B_AT, half) for half in range(2)]
    strip_c = [[strip(14 + field, C_AT + field, half) for half in range(2)] for field in range(4)]

    e = [{}, {}, {}, {}]
    strips = [[None, None] for _ in range(4)]
    reach = ((-1, 0), (-2, -1, 0, 1), (-1, 0, 1, 2), (0, 1, 2, 3))
    for step in range(4):
        last = step == 3
        rows = reach[step] + tuple(7 - row for row in reach[step])
        later = [{}, {}, {}, {}]
        later_strips = [[None, None] for _ in range(4)]
        for field in range(4):
            x = e[field]
            plane = step * 4 + field
            for half in range(2):
                xs = strips[field][half]
                if step > 0:
                    beside = ((DIFFUSION + strip_b[half]) * xs, (DIFFUSION - strip_b[half]) * xs)
                    rolled_right = pltpu.roll(beside[0], 127, 1)
                    rolled_left = pltpu.roll(beside[1], 1, 1)
                    inner = beside[0]
                for row in rows:
                    terms = []
                    if (row, half) in x:
                        here = x[row, half]
                        at = (row + 2) * 8
                        shares, pair = along(
                            here, right_weight(row, half), left_weight(row, half), beside, at, lane
                        )
                        local = CENTRE * here + shares
                        if field < 2:
                            local = local - (
                                couple(field, row, half) * e[2][row, half]
                                + couple(field + 2, row, half) * e[3][row, half]
                            )
                        terms.append(local)
                        if not last:
                            inner = insert(inner, pair, at, lane)
                    for near, crossing, weight in (
                        (row + 1, (0, 8), up_weight),
                        (row - 1, (-1, 7), down_weight),
                    ):
                        parts = []
                        if (near, half) in x:
                            parts.append(x[near, half])
                        if near in crossing:
                            parts.append(border_of[near](plane, half))
                        if parts:
                            terms.append(weight(near, half) * sum(parts[1:], parts[0]))
                    total = sum(terms[1:], terms[0])
                    if row == -1:
                        total = total * low_mask
                    if row == 8:
                        total = total * high_mask
                    if last:
                        total = total + own_ref[field, row, half * 8 : half * 8 + 8, :]
                        out_ref[field, pl.ds(half * 64 + row, 8, stride=8), :] = total
                    else:
                        later[field][row, half] = total
                if not last:
                    at = (plane * 2 + half) * 8
                    border = border_ref[at : at + 8, :]
                    from_above = jnp.where(jnp.logical_or(strip_row == 0, strip_row == 8), border, 0.0)
                    from_below = jnp.where(jnp.logical_or(strip_row == -1, strip_row == 7), border, 0.0)
                    if step > 0:
                        from_above, from_below = from_above + xs, from_below + xs
                    total = pltpu.roll((DIFFUSION + strip_a[half]) * from_above, 120, 1)
                    total = total + pltpu.roll((DIFFUSION - strip_a[half]) * from_below, 8, 1)
                    if step > 0:
                        total = total + CENTRE * xs + strip_along(rolled_right, rolled_left, inner, side)
                        if field < 2:
                            total = total - (
                                strip_c[field][half] * strips[2][half] + strip_c[field + 2][half] * strips[3][half]
                            )
                    later_strips[field][half] = total * strip_mask
        e, strips = later, later_strips


def vmem(count):
    return [pl.BlockSpec(memory_space=pltpu.VMEM)] * count


def params(mebibytes=24):
    return pltpu.CompilerParams(vmem_limit_bytes=mebibytes * 1024 * 1024)


def body(lam_end, winds, coupling, obs_values, obs_column, obs_count):
    bands = lax.axis_size("lat")
    tiles = lax.axis_size("lon")
    lam = lam_end.reshape(4, 128, 128)
    wind = winds.reshape(2, 128, 128)
    couple = coupling.reshape(4, 128, 128)

    lon_rows = (LON_ROWS, STRIP_ROW, LON_ROWS)
    parts = pl.pallas_call(
        pack_kernel,
        out_shape=tuple(jax.ShapeDtypeStruct((rows, 128), F32) for rows in lon_rows),
        in_specs=[pl.BlockSpec(memory_space=pltpu.HBM)] * 6,
        out_specs=tuple(vmem(3)),
        scratch_shapes=[
            pltpu.SMEM((1, 4), jnp.int32),
            pltpu.VMEM((4, 64), jnp.int32),
            pltpu.VMEM((4, 64, 128), F32),
            pltpu.VMEM((4, 128, 128), F32),
            pltpu.VMEM((2, 128, 128), F32),
            pltpu.VMEM((4, 128, 128), F32),
            pltpu.SemaphoreType.DMA((6,)),
        ],
        compiler_params=pltpu.CompilerParams(vmem_limit_bytes=54950 * 1024),
        name="pack_blocks_and_strips",
    )(obs_count, obs_column[0], obs_values[0], lam, wind, couple)
    got3, got2, got1 = [
        lax.ppermute(parts[apart - 1], "lon", [(i, i ^ apart) for i in range(tiles)]) for apart in (3, 2, 1)
    ]

    own_part = pl.pallas_call(
        own_blocks_kernel,
        out_shape=jax.ShapeDtypeStruct((STRIP_ROW, 128), F32),
        in_specs=[pl.BlockSpec(memory_space=pltpu.SMEM)] + vmem(2),
        out_specs=vmem(1)[0],
        compiler_params=params(),
        cost_estimate=pl.CostEstimate(flops=5_000_000, bytes_accessed=1_000_000, transcendentals=0),
        name="own_blocks",
    )(obs_count, obs_column[0], obs_values[0])

    halo = jax.ShapeDtypeStruct((LAT_ROWS, 128), F32)
    even, odd, force, strips = pl.pallas_call(
        halo_kernel,
        out_shape=(
            halo,
            halo,
            jax.ShapeDtypeStruct((8, 128, 128), F32),
            jax.ShapeDtypeStruct((128, 128), F32),
        ),
        in_specs=vmem(7),
        out_specs=tuple(vmem(4)),
        scratch_shapes=[pltpu.VMEM((128, 128), F32)],
        compiler_params=params(),
        name="scatter_and_halo",
    )(got2, got3, got1, own_part, lam, wind, couple)
    swap = lambda first: [p for i in range(first, bands - 1, 2) for p in ((i, i + 1), (i + 1, i))]
    got_odd = lax.ppermute(odd, "lat", swap(1))
    got_even = lax.ppermute(even, "lat", swap(0))

    own, wide = pl.pallas_call(
        own_kernel,
        out_shape=(jax.ShapeDtypeStruct((4, 8, 16, 128), F32), jax.ShapeDtypeStruct((288, 128), F32)),
        in_specs=vmem(5),
        out_specs=tuple(vmem(2)),
        compiler_params=params(),
        cost_estimate=pl.CostEstimate(flops=10_000_000, bytes_accessed=2_000_000, transcendentals=0),
        name="own_steps",
    )(force, strips, lam, wind, couple)

    out = pl.pallas_call(
        functools.partial(join_kernel, bands),
        out_shape=jax.ShapeDtypeStruct((4, 128, 128), F32),
        in_specs=vmem(8),
        out_specs=vmem(1)[0],
        scratch_shapes=[pltpu.VMEM((192, 128), F32)],
        compiler_params=params(),
        name="join_bands",
    )(got_odd, got_even, odd, even, own, wide, wind, couple)
    return out.reshape(lam_end.shape)


def solution(mesh):
    return jax.shard_map(
        body,
        mesh=mesh,
        in_specs=(
            P(None, None, "lat", "lon"),
            P(None, None, "lat", "lon"),
            P(None, None, "lat", "lon"),
            P(("lat", "lon"), None, None, None),
            P(("lat", "lon"), None, None),
            P(("lat", "lon"), None),
        ),
        out_specs=P(None, None, "lat", "lon"),
        check_vma=False,
    )
```
